128 devices in a mesh: exp: 8 (over z, core), pix: 16 (over x, y).
Axes of the slice: x: 4, y: 4, z: 4, core: 2. Of those that a mesh axis runs over, the one named last changes fastest.
Arguments:
- sky: bfloat16 [512, 512, 512], P('exp', 'pix'), may hold values from -6 to 6
- kernels: bfloat16 [6, 25, 25], replicated, may hold values from -0.25 to 0.25
- coefs: bfloat16 [32, 6, 512, 1536], P('exp', None, 'pix'), may hold values from 0.19921875 to 1
- observed: float32 [32, 512, 1536], P('exp', 'pix'), may hold values from -8 to 8
- inv_var: bfloat16 [32, 512, 1536], P('exp', 'pix'), may hold values from 0.25 to 4
- footprints: int32 [32, 8], replicated, may hold values from 0 to 511, as said below
- offsets: int32 [32, 2], replicated, may hold values from 0 to 500, as said below
- tile_slot: int32 [512], replicated, may hold values from 0 to 511, as said below
Outputs:
- sky_gradient: float32 [512, 512, 512], P('exp', 'pix')
The draws below stay inside these ranges and needn't reach their ends.
Inputs may be any that keep to these rules, and one draw needn't show every extreme that they name: `footprints`: exposure e reads tile row r and the row below it, columns c to c + 3 of the sky grid of 32 x 16 tiles (tile id = 16 row + column): entry 4 i + j is tile (r + i, c + j). Exposures are dealt to exp in blocks of 4. Column 0 is a row offset, a multiple of 32 below 512; the row offsets of the 4 exposures of one block differ from one another after division by 32. Column 1 is a column offset from 12 to 500. `tile_slot`: A permutation. The four tiles of one tile row of any footprint lie in four different blocks of 64 storage rows.
All inputs are finite; a program needn't handle non-finite values.
Results may differ from the reference program's by a relative error of at most 0.01.
Values may be sent and summed in bfloat16 or wider, within the bound.
A program may use at most 128 MiB of HBM per device.

```python
import math
import jax
import jax.numpy as jnp
from jax import lax

TILE = 512
KS = 25
NBASIS = 6
GRIDX = 16
EXP_G = 4
RIM = 12
EXPW = 1536
NTILES = 512
GRIDY = 32
NEXP = 32
N_EXP = 8
N_PIX = 16


def draw_footprints(key, part):
    key = jax.random.fold_in(key, 11)
    first, second = jax.random.split(key)
    top = jax.random.randint(first, (NEXP,), 0, GRIDY - 1)
    left = jax.random.randint(second, (NEXP,), 0, GRIDX - 3)
    top = top.at[0].set(GRIDY - 2)
    left = left.at[0].set(GRIDX - 4)
    down = jnp.array([0, 0, 0, 0, 1, 1, 1, 1], jnp.int32)
    across = jnp.array([0, 1, 2, 3, 0, 1, 2, 3], jnp.int32)
    return ((top[:, None] + down[None]) * GRIDX + left[:, None] + across[None]).astype(jnp.int32)


def draw_offsets(key, part):
    key = jax.random.fold_in(key, 12)
    first, second = jax.random.split(key)
    strip_rows = TILE // N_PIX
    scores = jax.random.randint(first, (N_EXP, N_PIX), 0, 1 << 20) * N_PIX + jnp.arange(N_PIX, dtype=jnp.int32)[None]
    phases = jnp.argsort(scores, axis=1)[:, :EXP_G]
    top = (phases * strip_rows).reshape(-1)
    left = jax.random.randint(second, (NEXP,), RIM, TILE - RIM + 1)
    left = left.at[0].set(TILE - RIM)
    left = left.at[1].set(RIM)
    return jnp.stack([top, left], axis=1).astype(jnp.int32)


def draw_tile_slot(key, part):
    key = jax.random.fold_in(key, 13)
    first, second = jax.random.split(key)
    turns = jax.random.randint(first, (GRIDY,), 0, N_EXP)
    index = jnp.arange(NTILES, dtype=jnp.int32)
    holder = (index % GRIDX + turns[index // GRIDX]) % N_EXP
    scores = holder * NTILES + jax.random.permutation(second, NTILES).astype(jnp.int32)
    order = jnp.argsort(scores)
    return jnp.argsort(order).astype(jnp.int32)


def block_levels(rng, extent, shards, least, high):
    gain, own = 1.0, jax.random.fold_in(rng, 6)
    for position, shards_of in shards:
        draws = jnp.exp(jax.random.uniform(jax.random.fold_in(own, position), (shards_of,), jnp.float32, least / len(shards), high / len(shards)))
        gain = gain * jnp.repeat(draws, extent[position] // shards_of).reshape([-1 if axis == position else 1 for axis in range(len(extent))])
    return gain


def gaussian(own_key, shape, width, limit, cuts=(), held_as=jnp.bfloat16):
    entries = jax.random.normal(own_key, shape, jnp.float32) * width
    if len(cuts) > 0:
        entries = block_levels(own_key, shape, cuts, -0.22, 0.18) * entries
    return jnp.clip(entries, min=-limit, max=limit).astype(held_as)


def setup_inputs(seed: int = 0) -> dict:
    key_of = jax.random.split(jax.random.key(seed), 9)
    return {
        "sky": gaussian(key_of[0], (NTILES, TILE, TILE), 1.0, 6.0, ((0, 8), (1, 16))),
        "kernels": gaussian(key_of[1], (NBASIS, KS, KS), (KS * KS) ** -0.5, 0.25),
        "coefs": jnp.clip(0.19921875 + 0.80078125 * jax.random.uniform(key_of[2], (NEXP, NBASIS, TILE, EXPW), jnp.float32) ** block_levels(key_of[2], (NEXP, NBASIS, TILE, EXPW), ((0, 8), (2, 16)), -0.2, 0.2), 0.19921875, 1.0).astype(jnp.bfloat16),
        "observed": gaussian(key_of[3], (NEXP, TILE, EXPW), 1.5, 8.0, ((0, 8), (1, 16)), jnp.float32),
        "inv_var": jnp.clip(jnp.exp(math.log(4.0) - 2.7725887 * jax.random.uniform(key_of[4], (NEXP, TILE, EXPW), jnp.float32) ** block_levels(key_of[4], (NEXP, TILE, EXPW), ((0, 8), (1, 16)), -0.2, 0.2)), 0.25, 4.0).astype(jnp.bfloat16),
        "footprints": draw_footprints(jax.random.fold_in(key_of[8], 71), 0),
        "offsets": draw_offsets(jax.random.fold_in(key_of[8], 71), 0),
        "tile_slot": draw_tile_slot(jax.random.fold_in(key_of[8], 71), 0),
    }


def reference(sky, kernels, coefs, observed, inv_var, footprints, offsets, tile_slot):
    margin = KS // 2
    upright = kernels[:, None]
    flipped = kernels[:, ::-1, ::-1][None]

    def visit(gradient, inputs):
        block, shift_pair, coef_field, seen, weight = inputs
        stored = tile_slot[block]
        tiles = sky[stored]
        assembled = tiles.reshape(2, 4, TILE, TILE).transpose(0, 2, 1, 3).reshape(2 * TILE, 4 * TILE)
        band = lax.dynamic_slice_in_dim(assembled, shift_pair[0], TILE, 0)
        band = jnp.pad(band, ((margin, margin), (0, 0)))
        window = lax.dynamic_slice_in_dim(band, shift_pair[1] - margin, EXPW + 2 * margin, 1)
        blurred = lax.conv_general_dilated(window[None, None], upright, (1, 1), "VALID", preferred_element_type=jnp.float32)[0]
        coef_wide = coef_field.astype(jnp.float32)
        model = jnp.sum(coef_wide * blurred, axis=0)
        resid = weight.astype(jnp.float32) * (model - seen)
        weighted = (coef_wide * resid[None]).astype(jnp.bfloat16)
        padding = ((2 * margin, 2 * margin), (2 * margin, 2 * margin))
        back = lax.conv_general_dilated(weighted[None], flipped, (1, 1), padding, preferred_element_type=jnp.float32)[0, 0]
        inner = back[margin:margin + TILE]
        canvas = jnp.zeros((2 * TILE, 4 * TILE), jnp.float32)
        placed = lax.dynamic_update_slice(canvas, inner, (shift_pair[0], shift_pair[1] - margin))
        pieces = placed.reshape(2, TILE, 4, TILE).transpose(0, 2, 1, 3).reshape(8, TILE, TILE).astype(jnp.bfloat16)
        pieces = lax.optimization_barrier(pieces)
        return gradient.at[stored].add(pieces.astype(jnp.float32)), None

    start = jnp.zeros((NTILES, TILE, TILE), jnp.float32)
    gradient, unused = lax.scan(visit, start, (footprints, offsets, coefs, observed, inv_var))
    return gradient
```

```python
import jax
import jax.numpy as jnp
from jax import lax
from jax.experimental import pallas as pl
from jax.experimental.pallas import tpu as pltpu
from jax.sharding import PartitionSpec as P


KS = 25
def tables(kernels):
    nb, ks, _ = kernels.shape
    rows, tall = 32, 64
    u = jnp.arange(ks)[:, None, None]; Y = jnp.arange(tall)[None, :, None]; y = jnp.arange(rows)[None, None, :]
    hot = (Y - 4 - y == u).astype(kernels.dtype)
    t = jnp.einsum("buv,uYy->bvYy", kernels, hot, preferred_element_type=jnp.float32).astype(kernels.dtype)
    fwd = t.transpose(0, 3, 1, 2).reshape(nb * rows, ks * tall)
    adj = t.reshape(nb, 5, 5, tall, rows).transpose(1, 3, 2, 0, 4).reshape(5 * tall, 5 * nb * rows)
    return fwd, adj

def blur_kernel(shift_ref, band_ref, coef_ref, obs_ref, inv_ref, fwd_ref, adj_ref, out_ref, stack, wide):
    q = pl.program_id(0)
    shift = shift_ref[q]
    W = 1536
    band = band_ref[0].astype(jnp.float32)
    width = band.shape[1]
    win = pltpu.roll(band, (width - shift) % width, axis=1)[:, :1664].astype(jnp.bfloat16)
    for v in range(KS):
        stack[v*64:(v+1)*64, :] = win[:, v:v+W]
    nc = 512
    for n in range(W // nc):
        cols = slice(n*nc, (n+1)*nc)
        blurred = jnp.dot(fwd_ref[...], stack[:, cols], preferred_element_type=jnp.float32)
        coef = [coef_ref[0, b, :, cols].astype(jnp.float32) for b in range(6)]
        model = coef[0] * blurred[0:32]
        for b in range(1, 6):
            model = model + coef[b] * blurred[b*32:(b+1)*32]
        resid = inv_ref[0, :, cols].astype(jnp.float32) * (model - obs_ref[0, :, cols])
        for b in range(6):
            wide[b*32:(b+1)*32, cols] = (coef[b] * resid).astype(jnp.bfloat16)
    wide[0:192, W:] = jnp.zeros((192, 128), jnp.bfloat16)
    base = wide[0:192, :]
    for c in range(1, 5):
        wide[c*192:(c+1)*192, :] = jnp.concatenate([jnp.zeros((192, c), jnp.bfloat16), base[:, :1664-c]], axis=1)
    part = jnp.dot(adj_ref[...], wide[...], preferred_element_type=jnp.float32)
    back = part[0:64]
    for a in range(1, 5):
        back = back + pltpu.roll(part[a*64:(a+1)*64], 5*a, axis=1)
    back = jnp.concatenate([back, jnp.zeros((64, width - 1664), jnp.float32)], axis=1)
    out_ref[0] = pltpu.roll(back, shift, axis=1).astype(out_ref.dtype)

def blur(shift, band, coefs, observed, inv_var, fwd, adj, out_dtype=jnp.float32):
    nv = band.shape[0]
    whole = lambda a: pl.BlockSpec(a.shape, lambda q, s: (0,)*a.ndim)
    per = lambda a: pl.BlockSpec((1,)+a.shape[1:], lambda q, s: (q,)+(0,)*(a.ndim-1))
    return pl.pallas_call(
        blur_kernel,
        grid_spec=pltpu.PrefetchScalarGridSpec(
            num_scalar_prefetch=1, grid=(nv,),
            in_specs=[per(band), per(coefs), per(observed), per(inv_var), whole(fwd), whole(adj)],
            out_specs=pl.BlockSpec((1,64,2048), lambda q, s: (q,0,0)),
            scratch_shapes=[pltpu.VMEM((1600,1536), jnp.bfloat16), pltpu.VMEM((960,1664), jnp.bfloat16)]),
        out_shape=jax.ShapeDtypeStruct((nv,64,2048), out_dtype),
        compiler_params=pltpu.CompilerParams(vmem_limit_bytes=50*2**20),
    )(shift, band, coefs, observed, inv_var, fwd, adj)


def with_halo(block, sides, width):
    for axis, dim in sides:
        count = lax.axis_size(axis)
        forward = [(i, i + 1) for i in range(count - 1)]
        backward = [(target, source) for source, target in forward]
        low = lax.ppermute(
            lax.slice_in_dim(block, block.shape[dim] - width, None, axis=dim), axis, forward
        )
        high = lax.ppermute(lax.slice_in_dim(block, 0, width, axis=dim), axis, backward)
        block = jnp.concatenate([low, block, high], axis=dim)
    return block


def passed_along(x, axis, by):
    peers = lax.axis_size(axis)
    pairs = [(i, i + by) for i in range(peers) if 0 <= i + by < peers]
    return lax.ppermute(x, axis, pairs)


def owned_rows(tiles, owner_of, local_of, group_index):
    belongs = owner_of[tiles] == group_index
    which = jnp.argmax(belongs.astype(jnp.int32), axis=-1)
    chosen = jnp.take_along_axis(tiles, which[..., None], axis=-1)[..., 0]
    return (local_of[chosen], jnp.any(belongs, axis=-1))


def local(sky, kernels, coefs, observed, inv_var, footprints, offsets, tile_slot):
    group_count = lax.axis_size("exp")
    strip_count = lax.axis_size("pix")
    group_index = lax.axis_index("exp")
    strip_index = lax.axis_index("pix")
    stored, strip_rows, tile_side = sky.shape
    visits = observed.shape[0]
    image_width = observed.shape[2]
    kernel_side = kernels.shape[1]
    basis_count = kernels.shape[0]
    margin = kernel_side // 2
    owner_of = tile_slot // stored
    local_of = tile_slot % stored
    blocks = footprints.reshape(group_count, visits, 2, 4)
    phases = (offsets[:, 0] // strip_rows).reshape(group_count, visits)
    shifts = offsets[:, 1].reshape(group_count, visits)
    my_phase = phases[group_index]
    my_shift = shifts[group_index]
    visit_range = jnp.arange(visits)
    strip_range = jnp.arange(strip_count)
    nothing = jnp.zeros((), sky.dtype)
    lower_row = strip_index < phases
    row_tiles = jnp.where(lower_row[..., None], blocks[:, :, 1], blocks[:, :, 0])
    held_rows, held = owned_rows(row_tiles, owner_of, local_of, group_index)
    outgoing = jnp.where(held[..., None, None], sky[held_rows], nothing)
    arrived = lax.all_to_all(outgoing, "exp", split_axis=0, concat_axis=0, tiled=True)
    source = owner_of[row_tiles[group_index]]
    picked = arrived[source, visit_range[:, None]]
    matching = (my_phase[None, :] + strip_range[:, None]) % strip_count == strip_index
    chosen = jnp.argmax(matching.astype(jnp.int32), axis=1)
    present = jnp.any(matching, axis=1)
    forward_rows = jnp.where(present[:, None, None, None], picked[chosen], nothing)
    landed = lax.all_to_all(forward_rows, "pix", split_axis=0, concat_axis=0, tiled=True)
    mine = landed[(my_phase + strip_index) % strip_count]
    band = mine.transpose(0, 2, 1, 3).reshape(visits, strip_rows, 4 * tile_side)
    padded = with_halo(band, (("pix", 1),), 16)

    fwd, adj = tables(kernels)
    back = blur(my_shift - margin, padded, coefs, observed, inv_var, fwd, adj)
    from_lower = passed_along(back[:, 48:].astype(jnp.bfloat16), "pix", 1).astype(jnp.float32)
    from_upper = passed_along(back[:, :16].astype(jnp.bfloat16), "pix", -1).astype(jnp.float32)
    placed = back[:, 16:48] + jnp.concatenate([from_lower, from_upper], axis=1)
    pieces = (
        placed.reshape(visits, strip_rows, 4, tile_side).transpose(0, 2, 1, 3).astype(jnp.bfloat16)
    )
    gradient = jnp.zeros((stored, strip_rows, tile_side), jnp.float32)
    back_match = (my_phase[None, :] + strip_index) % strip_count == strip_range[:, None]
    back_visit = jnp.argmax(back_match.astype(jnp.int32), axis=1)
    back_has = jnp.any(back_match, axis=1)
    to_rows = jnp.where(back_has[:, None, None, None], pieces[back_visit], nothing)
    gathered = lax.all_to_all(to_rows, "pix", split_axis=0, concat_axis=0, tiled=True)
    per_visit = gathered[(strip_index - my_phase) % strip_count]
    owners_row = owner_of[row_tiles[group_index]]
    selector = (owners_row[None] == jnp.arange(group_count)[:, None, None]).astype(jnp.bfloat16)
    to_owners = jnp.einsum(
        "gqj,qjst->gqst", selector, per_visit, preferred_element_type=jnp.float32
    ).astype(jnp.bfloat16)
    returned = lax.all_to_all(to_owners, "exp", split_axis=0, concat_axis=0, tiled=True)
    terms = jnp.where(held[..., None, None], returned.astype(jnp.float32), 0.0)
    gradient = gradient.at[held_rows.reshape(-1)].add(terms.reshape(-1, strip_rows, tile_side))
    return gradient


def solution(mesh):
    return jax.shard_map(
        local,
        mesh=mesh,
        in_specs=(
            P("exp", "pix", None),
            P(),
            P("exp", None, "pix", None),
            P("exp", "pix", None),
            P("exp", "pix", None),
            P(),
            P(),
            P(),
        ),
        out_specs=P("exp", "pix", None),
        check_vma=False,
    )
```

```python
import jax
import jax.numpy as jnp
from jax import lax
from jax.experimental import pallas as pl
from jax.experimental.pallas import tpu as pltpu
from jax.sharding import PartitionSpec as P

KS = 25
def tables(kernels):
    nb, ks, _ = kernels.shape
    rows, tall = 32, 64
    u = jnp.arange(ks)[:, None, None]; Y = jnp.arange(tall)[None, :, None]; y = jnp.arange(rows)[None, None, :]
    hot = (Y - 4 - y == u).astype(kernels.dtype)
    t = jnp.einsum("buv,uYy->bvYy", kernels, hot, preferred_element_type=jnp.float32).astype(kernels.dtype)
    fwd = t.transpose(0, 3, 1, 2).reshape(nb * rows, ks * tall)
    adj = t.reshape(nb, 5, 5, tall, rows).transpose(1, 3, 2, 0, 4).reshape(5 * tall, 5 * nb * rows)
    return fwd, adj

def blur_kernel(shift_ref, band_ref, coef_ref, obs_ref, inv_ref, fwd_ref, adj_ref, out_ref, stack, wide):
    q = pl.program_id(0)
    shift = shift_ref[q]
    W = 1536
    band = band_ref[0].astype(jnp.float32)
    width = band.shape[1]
    win = pltpu.roll(band, (width - shift) % width, axis=1)[:, :1664].astype(jnp.bfloat16)
    for v in range(KS):
        stack[v*64:(v+1)*64, :] = win[:, v:v+W]
    nc = 512
    for n in range(W // nc):
        cols = slice(n*nc, (n+1)*nc)
        blurred = jnp.dot(fwd_ref[...], stack[:, cols], preferred_element_type=jnp.float32)
        coef = [coef_ref[0, b, :, cols].astype(jnp.float32) for b in range(6)]
        model = coef[0] * blurred[0:32]
        for b in range(1, 6):
            model = model + coef[b] * blurred[b*32:(b+1)*32]
        resid = inv_ref[0, :, cols].astype(jnp.float32) * (model - obs_ref[0, :, cols])
        for b in range(6):
            wide[b*32:(b+1)*32, cols] = (coef[b] * resid).astype(jnp.bfloat16)
    wide[0:192, W:] = jnp.zeros((192, 128), jnp.bfloat16)
    base = wide[0:192, :]
    for c in range(1, 5):
        wide[c*192:(c+1)*192, :] = jnp.concatenate([jnp.zeros((192, c), jnp.bfloat16), base[:, :1664-c]], axis=1)
    part = jnp.dot(adj_ref[...], wide[...], preferred_element_type=jnp.float32)
    back = part[0:64]
    for a in range(1, 5):
        back = back + pltpu.roll(part[a*64:(a+1)*64], 5*a, axis=1)
    back = jnp.concatenate([back, jnp.zeros((64, width - 1664), jnp.float32)], axis=1)
    out_ref[0] = pltpu.roll(back, shift, axis=1).astype(out_ref.dtype)

def blur(shift, band, coefs, observed, inv_var, fwd, adj, out_dtype=jnp.float32):
    nv = band.shape[0]
    whole = lambda a: pl.BlockSpec(a.shape, lambda q, s: (0,)*a.ndim)
    per = lambda a: pl.BlockSpec((1,)+a.shape[1:], lambda q, s: (q,)+(0,)*(a.ndim-1))
    return pl.pallas_call(
        blur_kernel,
        grid_spec=pltpu.PrefetchScalarGridSpec(
            num_scalar_prefetch=1, grid=(nv,),
            in_specs=[per(band), per(coefs), per(observed), per(inv_var), whole(fwd), whole(adj)],
            out_specs=pl.BlockSpec((1,64,2048), lambda q, s: (q,0,0)),
            scratch_shapes=[pltpu.VMEM((1600,1536), jnp.bfloat16), pltpu.VMEM((960,1664), jnp.bfloat16)]),
        out_shape=jax.ShapeDtypeStruct((nv,64,2048), out_dtype),
        compiler_params=pltpu.CompilerParams(vmem_limit_bytes=50*2**20),
    )(shift, band, coefs, observed, inv_var, fwd, adj)


E_AXIS, P_AXIS = "exp", "pix"
MESH_ID = pl.DeviceIdType.MESH
GROUPS = ((0, 1), (2, 3))


def greet(me_e, me_p, ne, np_):
    barrier = pltpu.get_barrier_semaphore()
    for d in range(1, ne):
        pl.semaphore_signal(barrier, inc=1, device_id=(lax.rem(me_e + d, ne), me_p), device_id_type=MESH_ID)
    for d in range(1, np_):
        pl.semaphore_signal(barrier, inc=1, device_id=(me_e, lax.rem(me_p + d, np_)), device_id_type=MESH_ID)
    return lambda: pl.semaphore_wait(barrier, ne + np_ - 2)


def remote(src, dst, send, recv, device):
    return pltpu.make_async_remote_copy(
        src_ref=src, dst_ref=dst, send_sem=send, recv_sem=recv, device_id=device, device_id_type=MESH_ID
    )


def row_base(offs_ref, exposure, strip):
    phase = offs_ref[exposure, 0] >> 5
    return phase, jnp.where(strip < phase, 4, 0)


def gather_kernel(foot, offs, slots, sky, band, *scratch):
    ng = len(GROUPS)
    recv1, recv2 = scratch[0:ng], scratch[ng:2 * ng]
    stage1, stage2, stage3, s1, r1, s2, r2, s3, r3 = scratch[2 * ng:]
    ne, np_ = 8, 16
    me_e, me_p = lax.axis_index(E_AXIS), lax.axis_index(P_AXIS)
    arrived = greet(me_e, me_p, ne, np_)

    def fill(g, carry):
        for q in range(4):
            _, base = row_base(offs, 4 * g + q, me_p)
            local = jnp.int32(0)
            for j in range(4):
                slot = slots[foot[4 * g + q, base + j]]
                local = jnp.where((slot >> 6) == me_e, slot & 63, local)
            stage1[g, q] = sky[local]
        return carry

    lax.fori_loop(0, ne, fill, 0)
    arrived()
    first, second, third = [], [], []
    for n, group in enumerate(GROUPS):
        q0, nq = group[0], len(group)
        copies = []
        for d in range(1, ne):
            g = lax.rem(me_e + d, ne)
            o = lax.rem(me_e + ne - d, ne)
            out = remote(stage1.at[g, pl.ds(q0, nq)], recv1[n].at[me_e], s1.at[n, g], r1.at[n, me_e], (g, me_p))
            out.start()
            copies.append((out, remote(stage1.at[g, pl.ds(q0, nq)], recv1[n].at[o], s1.at[n, g], r1.at[n, o], (g, me_p))))
        recv1[n][me_e] = stage1[me_e, q0:q0 + nq]
        first.append(copies)
    for n, group in enumerate(GROUPS):
        q0, nq = group[0], len(group)
        for _, inward in first[n]:
            inward.wait_recv()
        for k, q in enumerate(group):
            e = 4 * me_e + q
            _, base = row_base(offs, e, me_p)
            for j in range(4):
                source = slots[foot[e, base + j]] >> 6
                tile = recv1[n][source, k]
                for c in range(4):
                    stage2[4 * j + c, q] = tile[:, c * 128:(c + 1) * 128]
        copies = []
        for d in range(1, np_):
            i = lax.rem(me_p + d, np_)
            o = lax.rem(me_p + np_ - d, np_)
            src = stage2.at[i, pl.ds(q0, nq)]
            out = remote(src, recv2[n].at[me_p], s2.at[n, i], r2.at[n, me_p], (me_e, i))
            out.start()
            copies.append((out, remote(src, recv2[n].at[o], s2.at[n, i], r2.at[n, o], (me_e, i))))
        recv2[n][me_p] = stage2[me_p, q0:q0 + nq]
        second.append(copies)
    mine = pl.ds(pl.multiple_of(me_p * 128, 128), 128)
    for n, group in enumerate(GROUPS):
        q0, nq = group[0], len(group)
        for _, inward in second[n]:
            inward.wait_recv()
        for k, q in enumerate(group):
            phase = offs[4 * me_e + q, 0] >> 5
            for to in range(np_):
                strip = (phase + to) & 15
                stage3[to, q, 16:48] = recv2[n][strip, k]
                if to > 0:
                    stage3[to, q, 0:16] = recv2[n][(strip + 15) & 15, k, 16:32]
                else:
                    stage3[to, q, 0:16] = jnp.zeros((16, 128), jnp.bfloat16)
                if to < np_ - 1:
                    stage3[to, q, 48:64] = recv2[n][(strip + 1) & 15, k, 0:16]
                else:
                    stage3[to, q, 48:64] = jnp.zeros((16, 128), jnp.bfloat16)
        copies = []
        for d in range(1, np_):
            i = lax.rem(me_p + d, np_)
            o = lax.rem(me_p + np_ - d, np_)
            theirs = pl.ds(pl.multiple_of(o * 128, 128), 128)
            src = stage3.at[i, pl.ds(q0, nq)]
            out = remote(src, band.at[pl.ds(q0, nq), :, mine], s3.at[n, i], r3.at[n, me_p], (me_e, i))
            out.start()
            copies.append((out, remote(src, band.at[pl.ds(q0, nq), :, theirs], s3.at[n, i], r3.at[n, o], (me_e, i))))
        band[q0:q0 + nq, :, mine] = stage3[me_p, q0:q0 + nq]
        third.append(copies)
    for copies in third:
        for _, inward in copies:
            inward.wait_recv()
    for copies in first + second + third:
        for out, _ in copies:
            out.wait_send()


def gather_bands(footprints, offsets, tile_slot, sky):
    ng = len(GROUPS)
    bf = jnp.bfloat16
    dma = pltpu.SemaphoreType.DMA
    smem = pl.BlockSpec(memory_space=pltpu.SMEM)
    vmem = pl.BlockSpec(memory_space=pltpu.VMEM)
    return pl.pallas_call(
        gather_kernel,
        out_shape=jax.ShapeDtypeStruct((4, 64, 2048), bf),
        in_specs=[smem, smem, smem, vmem],
        out_specs=vmem,
        scratch_shapes=[pltpu.VMEM((8, len(g), 32, 512), bf) for g in GROUPS]
        + [pltpu.VMEM((16, len(g), 32, 128), bf) for g in GROUPS]
        + [pltpu.VMEM((8, 4, 32, 512), bf), pltpu.VMEM((16, 4, 32, 128), bf), pltpu.VMEM((16, 4, 64, 128), bf)]
        + [dma((ng, 8)), dma((ng, 8))] + [dma((ng, 16))] * 4,
        compiler_params=pltpu.CompilerParams(collective_id=0, has_side_effects=True, vmem_limit_bytes=40 * 2**20),
        name="gather_bands",
    )(footprints, offsets, tile_slot, sky)


def scatter_kernel(foot, offs, slots, back, pieces, *scratch):
    ng = len(GROUPS)
    recv1, recv2 = scratch[0:ng], scratch[ng:2 * ng]
    stage2, stage3, s1, r1, s2, r2, s3, r3 = scratch[2 * ng:]
    ne, np_ = 8, 16
    me_e, me_p = lax.axis_index(E_AXIS), lax.axis_index(P_AXIS)
    greet(me_e, me_p, ne, np_)()
    mine = pl.ds(pl.multiple_of(me_p * 128, 128), 128)
    first, second, third = [], [], []
    for n, group in enumerate(GROUPS):
        q0, nq = group[0], len(group)
        copies = []
        for d in range(1, np_):
            i = lax.rem(me_p + d, np_)
            o = lax.rem(me_p + np_ - d, np_)
            src = back.at[pl.ds(q0, nq), :, pl.ds(pl.multiple_of(i * 128, 128), 128)]
            out = remote(src, recv1[n].at[me_p], s1.at[n, i], r1.at[n, me_p], (me_e, i))
            out.start()
            copies.append((out, remote(src, recv1[n].at[o], s1.at[n, i], r1.at[n, o], (me_e, i))))
        recv1[n][me_p] = back[q0:q0 + nq, :, mine]
        first.append(copies)
    for n, group in enumerate(GROUPS):
        q0, nq = group[0], len(group)
        for _, inward in first[n]:
            inward.wait_recv()
        for k, q in enumerate(group):
            phase = offs[4 * me_e + q, 0] >> 5
            for to in range(np_):
                strip = (to - phase) & 15
                centre = recv1[n][strip, k, 16:48].astype(jnp.float32)
                above = recv1[n][(strip + 15) & 15, k, 48:64].astype(jnp.float32)
                below = recv1[n][(strip + 1) & 15, k, 0:16].astype(jnp.float32)
                above = jnp.where(strip > 0, above, 0.0)
                below = jnp.where(strip < np_ - 1, below, 0.0)
                stage2[to, q, 0:16] = (centre[0:16] + above).astype(jnp.bfloat16)
                stage2[to, q, 16:32] = (centre[16:32] + below).astype(jnp.bfloat16)
        copies = []
        for d in range(1, np_):
            i = lax.rem(me_p + d, np_)
            o = lax.rem(me_p + np_ - d, np_)
            src = stage2.at[i, pl.ds(q0, nq)]
            out = remote(src, recv2[n].at[me_p], s2.at[n, i], r2.at[n, me_p], (me_e, i))
            out.start()
            copies.append((out, remote(src, recv2[n].at[o], s2.at[n, i], r2.at[n, o], (me_e, i))))
        recv2[n][me_p] = stage2[me_p, q0:q0 + nq]
        second.append(copies)
    for n, group in enumerate(GROUPS):
        q0, nq = group[0], len(group)
        for _, inward in second[n]:
            inward.wait_recv()
        for k, q in enumerate(group):
            e = 4 * me_e + q
            _, base = row_base(offs, e, me_p)
            source = [slots[foot[e, base + j]] >> 6 for j in range(4)]
            for o in range(ne):
                which = jnp.int32(0)
                for j in range(1, 4):
                    which = jnp.where(source[j] == o, j, which)
                for c in range(4):
                    stage3[o, q, :, c * 128:(c + 1) * 128] = recv2[n][4 * which + c, k]
        copies = []
        for d in range(1, ne):
            g = lax.rem(me_e + d, ne)
            o = lax.rem(me_e + ne - d, ne)
            src = stage3.at[g, pl.ds(q0, nq)]
            out = remote(src, pieces.at[me_e, pl.ds(q0, nq)], s3.at[n, g], r3.at[n, me_e], (g, me_p))
            out.start()
            copies.append((out, remote(src, pieces.at[o, pl.ds(q0, nq)], s3.at[n, g], r3.at[n, o], (g, me_p))))
        pieces[me_e, q0:q0 + nq] = stage3[me_e, q0:q0 + nq]
        third.append(copies)
    for copies in third:
        for _, inward in copies:
            inward.wait_recv()
    for copies in first + second + third:
        for out, _ in copies:
            out.wait_send()


def scatter_pieces(footprints, offsets, tile_slot, back):
    ng = len(GROUPS)
    bf = jnp.bfloat16
    dma = pltpu.SemaphoreType.DMA
    smem = pl.BlockSpec(memory_space=pltpu.SMEM)
    vmem = pl.BlockSpec(memory_space=pltpu.VMEM)
    return pl.pallas_call(
        scatter_kernel,
        out_shape=jax.ShapeDtypeStruct((8, 4, 32, 512), bf),
        in_specs=[smem, smem, smem, vmem],
        out_specs=vmem,
        scratch_shapes=[pltpu.VMEM((16, len(g), 64, 128), bf) for g in GROUPS]
        + [pltpu.VMEM((16, len(g), 32, 128), bf) for g in GROUPS]
        + [pltpu.VMEM((16, 4, 32, 128), bf), pltpu.VMEM((8, 4, 32, 512), bf)]
        + [dma((ng, 16))] * 4 + [dma((ng, 8)), dma((ng, 8))],
        compiler_params=pltpu.CompilerParams(collective_id=1, has_side_effects=True, vmem_limit_bytes=40 * 2**20),
        name="scatter_pieces",
    )(footprints, offsets, tile_slot, back)


def total_kernel(foot, offs, slots, pieces, out):
    me_e, me_p = lax.axis_index(E_AXIS), lax.axis_index(P_AXIS)

    def clear(r, carry):
        out[r] = jnp.zeros(out.shape[1:], jnp.float32)
        return carry

    lax.fori_loop(0, out.shape[0], clear, 0)

    def add(g, carry):
        for q in range(4):
            _, base = row_base(offs, 4 * g + q, me_p)
            local, held = jnp.int32(0), jnp.int32(0)
            for j in range(4):
                slot = slots[foot[4 * g + q, base + j]]
                local = jnp.where((slot >> 6) == me_e, slot & 63, local)
                held = jnp.where((slot >> 6) == me_e, 1, held)

            @pl.when(held == 1)
            def _():
                out[local] = out[local] + pieces[g, q].astype(jnp.float32)
        return carry

    lax.fori_loop(0, 8, add, 0)


def total(footprints, offsets, tile_slot, pieces):
    smem = pl.BlockSpec(memory_space=pltpu.SMEM)
    vmem = pl.BlockSpec(memory_space=pltpu.VMEM)
    return pl.pallas_call(
        total_kernel,
        out_shape=jax.ShapeDtypeStruct((64, 32, 512), jnp.float32),
        in_specs=[smem, smem, smem, vmem],
        out_specs=vmem,
        compiler_params=pltpu.CompilerParams(vmem_limit_bytes=40 * 2**20),
        name="total",
    )(footprints, offsets, tile_slot, pieces)


def local(sky, kernels, coefs, observed, inv_var, footprints, offsets, tile_slot):
    shift = lax.dynamic_slice_in_dim(offsets[:, 1], 4 * lax.axis_index(E_AXIS), 4) - 12
    fwd, adj = tables(kernels)
    band = gather_bands(footprints, offsets, tile_slot, sky)
    back = blur(shift, band, coefs, observed, inv_var, fwd, adj, jnp.bfloat16)
    pieces = scatter_pieces(footprints, offsets, tile_slot, back)
    return total(footprints, offsets, tile_slot, pieces)


def solution(mesh):
    return jax.shard_map(
        local,
        mesh=mesh,
        in_specs=(
            P("exp", "pix", None),
            P(),
            P("exp", None, "pix", None),
            P("exp", "pix", None),
            P("exp", "pix", None),
            P(),
            P(),
            P(),
        ),
        out_specs=P("exp", "pix", None),
        check_vma=False,
    )
```

```python
import jax
import jax.numpy as jnp
from jax import lax
from jax.experimental import pallas as pl
from jax.experimental.pallas import tpu as pltpu
from jax.sharding import PartitionSpec as P

E_AXIS, P_AXIS = "exp", "pix"
MESH_ID = pl.DeviceIdType.MESH
KS, NB, RIM, NV = 25, 6, 12, 4
NE, NP = 8, 16
ROWS, TALL, LANES = 32, 64, 128
WIDTH, SPAN, FULL = 1536, 1664, 2048
BF, F32 = jnp.bfloat16, jnp.float32


def tables_kernel(kt, fwd, adj):
    lane = lax.broadcasted_iota(jnp.int32, (ROWS, LANES), 1)
    tail = {}
    for m in range(13):
        blocks = []
        for b in range(NB):
            low = pltpu.roll(jnp.broadcast_to(kt[b, 2 * m:2 * m + 1, :], (ROWS, LANES)), 0, axis=1, stride=1, stride_axis=0)
            if 2 * m + 1 < KS:
                high = pltpu.roll(
                    jnp.broadcast_to(kt[b, 2 * m + 1:2 * m + 2, :], (ROWS, LANES)), TALL, axis=1, stride=1, stride_axis=0
                )
                block = jnp.where(lane < TALL, low, high)
                fwd[b * ROWS:(b + 1) * ROWS, m * LANES:(m + 1) * LANES] = block.astype(BF)
            else:
                block = low
                fwd[b * ROWS:(b + 1) * ROWS, m * LANES:m * LANES + TALL] = block[:, :TALL].astype(BF)
            blocks.append(block)
        turned_a = jnp.concatenate(blocks[:4], axis=0).T
        turned_b = jnp.concatenate(blocks[4:] + [jnp.zeros((2 * ROWS, LANES), F32)], axis=0).T
        for h in range(2):
            v = 2 * m + h
            if v < KS:
                a, c = divmod(v, 5)
                adj[a * TALL:(a + 1) * TALL, c * LANES:(c + 1) * LANES] = turned_a[h * TALL:(h + 1) * TALL].astype(BF)
                tail[a, c] = turned_b[h * TALL:(h + 1) * TALL]
    wide_lane = lax.broadcasted_iota(jnp.int32, (TALL, LANES), 1)
    for a in range(5):
        for c in (0, 2):
            pair = jnp.where(wide_lane < 64, tail[a, c], pltpu.roll(tail[a, c + 1], 64, axis=1))
            adj[a * TALL:(a + 1) * TALL, 640 + c * 64:640 + c * 64 + LANES] = pair.astype(BF)
        adj[a * TALL:(a + 1) * TALL, 896:960] = tail[a, 4][:, :64].astype(BF)


def tables(kernels):
    kt = jnp.pad(kernels.transpose(0, 2, 1).astype(F32), ((0, 0), (0, 0), (4, LANES - KS - 4)))
    vmem = pl.BlockSpec(memory_space=pltpu.VMEM)
    return pl.pallas_call(
        tables_kernel,
        out_shape=(jax.ShapeDtypeStruct((NB * ROWS, KS * TALL), BF), jax.ShapeDtypeStruct((5 * TALL, 5 * NB * ROWS), BF)),
        in_specs=[vmem],
        out_specs=(vmem, vmem),
        compiler_params=pltpu.CompilerParams(vmem_limit_bytes=30 * 2**20),
        name="tables",
    )(kt)


def blur_step(q, shift, band, coef_ref, obs_ref, inv_ref, fwd, adj, stack, wide, back_ref):
    win = pltpu.roll(band[q].astype(F32), (FULL - shift) & (FULL - 1), axis=1)[:, :SPAN].astype(BF)
    for v in range(KS):
        stack[v * TALL:(v + 1) * TALL, :] = win[:, v:v + WIDTH]
    nc = 512
    wide[0:128, WIDTH:] = jnp.zeros((128, SPAN - WIDTH), BF)
    wide[640:704, WIDTH:] = jnp.zeros((64, SPAN - WIDTH), BF)

    def chunk(n, carry):
        cols = pl.ds(pl.multiple_of(n * nc, nc), nc)
        blurred = jnp.dot(fwd[...], stack[:, cols], preferred_element_type=F32)
        coef = [coef_ref[q, b, :, cols].astype(F32) for b in range(NB)]
        model = coef[0] * blurred[0:ROWS]
        for b in range(1, NB):
            model = model + coef[b] * blurred[b * ROWS:(b + 1) * ROWS]
        resid = inv_ref[q, :, cols].astype(F32) * (model - obs_ref[q, :, cols])
        for b in range(NB):
            at = b * ROWS if b < 4 else 640 + (b - 4) * ROWS
            wide[at:at + ROWS, cols] = (coef[b] * resid).astype(BF)
        return carry

    lax.fori_loop(0, WIDTH // nc, chunk, 0)
    head, rest = wide[0:128, :], wide[640:704, :]
    for c in range(1, 5):
        wide[c * 128:(c + 1) * 128, :] = jnp.concatenate([jnp.zeros((128, c), BF), head[:, :SPAN - c]], axis=1)
        wide[640 + c * 64:640 + (c + 1) * 64, :] = jnp.concatenate([jnp.zeros((64, c), BF), rest[:, :SPAN - c]], axis=1)
    part = jnp.dot(adj[...], wide[...], preferred_element_type=F32)
    back = part[0:TALL]
    for a in range(1, 5):
        back = back + pltpu.roll(part[a * TALL:(a + 1) * TALL], 5 * a, axis=1)
    back = jnp.concatenate([back, jnp.zeros((TALL, FULL - SPAN), F32)], axis=1)
    back_ref[q] = pltpu.roll(back, shift, axis=1).astype(BF)


def fused_kernel(foot, offs, slots, sky_hbm, coefs_hbm, obs_hbm, inv_hbm, fwd, adj, pieces, *scratch):
    recv1, recv2, recv4, recv5 = (scratch[4 * k:4 * k + 4] for k in range(4))
    (sky, coef, obs, inv, stage1, stage2, stage3, stage5, stage6, band, back, stack, wide,
     s1, r1, s2, r2, s3, r3, s4, r4, s5, r5, s6, r6, loads) = scratch[16:]
    me_e, me_p = lax.axis_index(E_AXIS), lax.axis_index(P_AXIS)
    barrier = pltpu.get_barrier_semaphore()
    for d in range(1, NE):
        pl.semaphore_signal(barrier, inc=1, device_id=(lax.rem(me_e + d, NE), me_p), device_id_type=MESH_ID)
    for d in range(1, NP):
        pl.semaphore_signal(barrier, inc=1, device_id=(me_e, lax.rem(me_p + d, NP)), device_id_type=MESH_ID)
    sky_load = pltpu.make_async_copy(sky_hbm, sky, loads.at[0])
    sky_load.start()
    rest_loads = [
        pltpu.make_async_copy(src, dst, loads.at[k])
        for k, (src, dst) in enumerate(((coefs_hbm, coef), (obs_hbm, obs), (inv_hbm, inv)), 1)
    ]
    for load in rest_loads:
        load.start()
    sky_load.wait()

    def base_of(exposure):
        return jnp.where(me_p < (offs[exposure, 0] >> 5), 4, 0)

    def fill(g, carry):
        for q in range(NV):
            base = base_of(4 * g + q)
            local = jnp.int32(0)
            for j in range(4):
                slot = slots[foot[4 * g + q, base + j]]
                local = jnp.where((slot >> 6) == me_e, slot & 63, local)
            stage1[g, q] = sky[local]
        return carry

    lax.fori_loop(0, NE, fill, 0)
    phase = [offs[4 * me_e + q, 0] >> 5 for q in range(NV)]
    shift = [offs[4 * me_e + q, 1] - RIM for q in range(NV)]
    source = []
    for q in range(NV):
        base = base_of(4 * me_e + q)
        source.append([slots[foot[4 * me_e + q, base + j]] >> 6 for j in range(4)])
    pl.semaphore_wait(barrier, NE + NP - 2)

    sent = []

    def exchange(count, me, device, src, dst, send, recv):
        inward = []
        for d in range(1, count):
            to, of = lax.rem(me + d, count), lax.rem(me + count - d, count)
            make = lambda slot, sem: pltpu.make_async_remote_copy(
                src_ref=src(to), dst_ref=dst(slot), send_sem=send.at[to], recv_sem=recv.at[sem],
                device_id=device(to), device_id_type=MESH_ID)
            out = make(me, me)
            out.start()
            sent.append(out)
            inward.append(make(of, of))
        return inward

    over_e, over_p = (lambda to: (to, me_p)), (lambda to: (me_e, to))

    def lanes(i):
        return pl.ds(pl.multiple_of(i * LANES, LANES), LANES)

    def arrive(copies):
        for copy in copies:
            copy.wait_recv()

    def step1(q):
        recv1[q][me_e] = stage1[me_e, q]
        return exchange(NE, me_e, over_e, lambda to: stage1.at[to, q], lambda i: recv1[q].at[i], s1.at[q], r1.at[q])

    def step2(q):
        for j in range(4):
            tile = recv1[q][source[q][j]]
            for c in range(4):
                stage2[4 * j + c, q] = tile[:, c * LANES:(c + 1) * LANES]
        recv2[q][me_p] = stage2[me_p, q]
        return exchange(NP, me_p, over_p, lambda to: stage2.at[to, q], lambda i: recv2[q].at[i], s2.at[q], r2.at[q])

    def step3(q):
        for to in range(NP):
            strip = (phase[q] + to) & 15
            stage3[to, q, 16:48] = recv2[q][strip]
            if to > 0:
                stage3[to, q, 0:16] = recv2[q][(strip + 15) & 15, 16:32]
            else:
                stage3[to, q, 0:16] = jnp.zeros((16, LANES), BF)
            if to < NP - 1:
                stage3[to, q, 48:64] = recv2[q][(strip + 1) & 15, 0:16]
            else:
                stage3[to, q, 48:64] = jnp.zeros((16, LANES), BF)
        band[q, :, lanes(me_p)] = stage3[me_p, q]
        return exchange(NP, me_p, over_p, lambda to: stage3.at[to, q], lambda i: band.at[q, :, lanes(i)], s3.at[q], r3.at[q])

    def step4(q):
        blur_step(q, shift[q], band, coef, obs, inv, fwd, adj, stack, wide, back)
        recv4[q][me_p] = back[q, :, lanes(me_p)]
        return exchange(NP, me_p, over_p, lambda to: back.at[q, :, lanes(to)], lambda i: recv4[q].at[i], s4.at[q], r4.at[q])

    def step5(q):
        for to in range(NP):
            strip = (to - phase[q]) & 15
            centre = recv4[q][strip, 16:48].astype(F32)
            above = jnp.where(strip > 0, recv4[q][(strip + 15) & 15, 48:64].astype(F32), 0.0)
            below = jnp.where(strip < NP - 1, recv4[q][(strip + 1) & 15, 0:16].astype(F32), 0.0)
            stage5[to, q, 0:16] = (centre[0:16] + above).astype(BF)
            stage5[to, q, 16:32] = (centre[16:32] + below).astype(BF)
        recv5[q][me_p] = stage5[me_p, q]
        return exchange(NP, me_p, over_p, lambda to: stage5.at[to, q], lambda i: recv5[q].at[i], s5.at[q], r5.at[q])

    def step6(q):
        for o in range(NE):
            which = jnp.int32(0)
            for j in range(1, 4):
                which = jnp.where(source[q][j] == o, j, which)
            for c in range(4):
                stage6[o, q, :, c * LANES:(c + 1) * LANES] = recv5[q][4 * which + c]
        pieces[me_e, q] = stage6[me_e, q]
        return exchange(NE, me_e, over_e, lambda to: stage6.at[to, q], lambda i: pieces.at[i, q], s6.at[q], r6.at[q])

    steps = (step1, step2, step3, step4, step5, step6)
    order = ORDER
    waiting = {}
    loaded = False
    for n, q in order:
        if n > 1:
            arrive(waiting.pop((n - 1, q)))
        if n == 4 and not loaded:
            for load in rest_loads:
                load.wait()
            loaded = True
        waiting[n, q] = steps[n - 1](q)
    for q in range(NV):
        arrive(waiting.pop((6, q)))
    for out in sent:
        out.wait_send()


ORDER = (
    (1, 0), (1, 1), (1, 2), (1, 3), (2, 0), (2, 1), (3, 0), (2, 2), (3, 1), (2, 3), (3, 2), (4, 0), (3, 3), (4, 1), (5, 0),
    (4, 2), (5, 1), (6, 0), (4, 3), (5, 2), (6, 1), (5, 3), (6, 2), (6, 3),
)


def fused(footprints, offsets, tile_slot, sky, coefs, observed, inv_var, fwd, adj):
    dma = pltpu.SemaphoreType.DMA
    smem = pl.BlockSpec(memory_space=pltpu.SMEM)
    vmem = pl.BlockSpec(memory_space=pltpu.VMEM)
    hbm = pl.BlockSpec(memory_space=pl.ANY)
    shapes = [(NE, ROWS, 512)] * 4 + [(NP, ROWS, LANES)] * 4 + [(NP, TALL, LANES)] * 4 + [(NP, ROWS, LANES)] * 4
    return pl.pallas_call(
        fused_kernel,
        out_shape=jax.ShapeDtypeStruct((NE, NV, ROWS, 512), BF),
        in_specs=[smem, smem, smem, hbm, hbm, hbm, hbm, vmem, vmem],
        out_specs=vmem,
        scratch_shapes=[pltpu.VMEM(s, BF) for s in shapes]
        + [
            pltpu.VMEM(sky.shape, BF),
            pltpu.VMEM(coefs.shape, BF),
            pltpu.VMEM(observed.shape, F32),
            pltpu.VMEM(inv_var.shape, BF),
            pltpu.VMEM((NE, NV, ROWS, 512), BF),
            pltpu.VMEM((NP, NV, ROWS, LANES), BF),
            pltpu.VMEM((NP, NV, TALL, LANES), BF),
            pltpu.VMEM((NP, NV, ROWS, LANES), BF),
            pltpu.VMEM((NE, NV, ROWS, 512), BF),
            pltpu.VMEM((NV, TALL, FULL), BF),
            pltpu.VMEM((NV, TALL, FULL), BF),
            pltpu.VMEM((KS * TALL, WIDTH), BF),
            pltpu.VMEM((5 * NB * ROWS, SPAN), BF),
        ]
        + [dma((NV, NE))] * 2 + [dma((NV, NP))] * 8 + [dma((NV, NE))] * 2 + [dma((4,))],
        compiler_params=pltpu.CompilerParams(collective_id=0, has_side_effects=True, vmem_limit_bytes=50 * 2**20),
        name="fused",
    )(footprints, offsets, tile_slot, sky, coefs, observed, inv_var, fwd, adj)


def total_kernel(foot, offs, slots, pieces, out):
    me_e, me_p = lax.axis_index(E_AXIS), lax.axis_index(P_AXIS)

    def clear(r, carry):
        out[r] = jnp.zeros(out.shape[1:], F32)
        return carry

    lax.fori_loop(0, out.shape[0], clear, 0)

    def add(g, carry):
        for q in range(NV):
            base = jnp.where(me_p < (offs[4 * g + q, 0] >> 5), 4, 0)
            local, held = jnp.int32(0), jnp.int32(0)
            for j in range(4):
                slot = slots[foot[4 * g + q, base + j]]
                local = jnp.where((slot >> 6) == me_e, slot & 63, local)
                held = jnp.where((slot >> 6) == me_e, 1, held)

            @pl.when(held == 1)
            def _():
                out[local] = out[local] + pieces[g, q].astype(F32)
        return carry

    lax.fori_loop(0, NE, add, 0)


def total(footprints, offsets, tile_slot, pieces, shape):
    smem = pl.BlockSpec(memory_space=pltpu.SMEM)
    vmem = pl.BlockSpec(memory_space=pltpu.VMEM)
    return pl.pallas_call(
        total_kernel,
        out_shape=jax.ShapeDtypeStruct(shape, F32),
        in_specs=[smem, smem, smem, vmem],
        out_specs=vmem,
        compiler_params=pltpu.CompilerParams(vmem_limit_bytes=40 * 2**20),
        name="total",
    )(footprints, offsets, tile_slot, pieces)


def local(sky, kernels, coefs, observed, inv_var, footprints, offsets, tile_slot):
    fwd, adj = tables(kernels)
    pieces = fused(footprints, offsets, tile_slot, sky, coefs, observed, inv_var, fwd, adj)
    return total(footprints, offsets, tile_slot, pieces, sky.shape)


def solution(mesh):
    return jax.shard_map(
        local,
        mesh=mesh,
        in_specs=(
            P("exp", "pix", None),
            P(),
            P("exp", None, "pix", None),
            P("exp", "pix", None),
            P("exp", "pix", None),
            P(),
            P(),
            P(),
        ),
        out_specs=P("exp", "pix", None),
        check_vma=False,
    )
```

```python
import jax
import jax.numpy as jnp
from jax import lax
from jax.experimental import pallas as pl
from jax.experimental.pallas import tpu as pltpu
from jax.sharding import PartitionSpec as P

E_AXIS, P_AXIS = "exp", "pix"
MESH_ID = pl.DeviceIdType.MESH
KS, NB, RIM, NV = 25, 6, 12, 4
NE, NP = 8, 16
ROWS, TALL, LANES = 32, 64, 128
WIDTH, SPAN, FULL, NCH = 1536, 1664, 2048, 13
BF, F32 = jnp.bfloat16, jnp.float32


def build_tables(kernels, kt, fwd, adj):
    lane = lax.broadcasted_iota(jnp.int32, (ROWS, LANES), 1)
    for b in range(NB):
        square = jnp.concatenate([kernels[b].astype(F32), jnp.zeros((KS, LANES - KS), F32)], axis=1)
        square = jnp.concatenate([square, jnp.zeros((LANES - KS, LANES), F32)], axis=0)
        kt[b] = pltpu.roll(square.T[0:ROWS], 4, axis=1)
    tail = {}
    for m in range(13):
        blocks = []
        for b in range(NB):
            low = pltpu.roll(jnp.broadcast_to(kt[b, 2 * m:2 * m + 1, :], (ROWS, LANES)), 0, axis=1, stride=1, stride_axis=0)
            if 2 * m + 1 < KS:
                high = pltpu.roll(
                    jnp.broadcast_to(kt[b, 2 * m + 1:2 * m + 2, :], (ROWS, LANES)), TALL, axis=1, stride=1, stride_axis=0
                )
                block = jnp.where(lane < TALL, low, high)
                fwd[b * ROWS:(b + 1) * ROWS, m * LANES:(m + 1) * LANES] = block.astype(BF)
            else:
                block = low
                fwd[b * ROWS:(b + 1) * ROWS, m * LANES:m * LANES + TALL] = block[:, :TALL].astype(BF)
            blocks.append(block)
        turned_a = jnp.concatenate(blocks[:4], axis=0).T
        turned_b = jnp.concatenate(blocks[4:] + [jnp.zeros((2 * ROWS, LANES), F32)], axis=0).T
        for h in range(2):
            v = 2 * m + h
            if v < KS:
                a, c = divmod(v, 5)
                adj[a * TALL:(a + 1) * TALL, c * LANES:(c + 1) * LANES] = turned_a[h * TALL:(h + 1) * TALL].astype(BF)
                tail[a, c] = turned_b[h * TALL:(h + 1) * TALL]
    wide_lane = lax.broadcasted_iota(jnp.int32, (TALL, LANES), 1)
    for a in range(5):
        for c in (0, 2):
            pair = jnp.where(wide_lane < 64, tail[a, c], pltpu.roll(tail[a, c + 1], 64, axis=1))
            adj[a * TALL:(a + 1) * TALL, 640 + c * 64:640 + c * 64 + LANES] = pair.astype(BF)
        adj[a * TALL:(a + 1) * TALL, 896:960] = tail[a, 4][:, :64].astype(BF)


def chunk_of(device, turn):
    return lax.rem(device + 2 * NP - turn, NP)


def forward_step(q, band, coef_ref, obs_ref, inv_ref, fwd, stack, wide):
    win = jnp.concatenate([band[c, q] for c in range(NCH)], axis=1)
    for v in range(KS):
        stack[v * TALL:(v + 1) * TALL, :] = win[:, v:v + WIDTH]
    nc = 512
    wide[0:128, WIDTH:] = jnp.zeros((128, SPAN - WIDTH), BF)
    wide[640:704, WIDTH:] = jnp.zeros((64, SPAN - WIDTH), BF)

    def chunk(n, carry):
        cols = pl.ds(pl.multiple_of(n * nc, nc), nc)
        blurred = jnp.dot(fwd[...], stack[:, cols], preferred_element_type=F32)
        coef = [coef_ref[q, b, :, cols].astype(F32) for b in range(NB)]
        model = coef[0] * blurred[0:ROWS]
        for b in range(1, NB):
            model = model + coef[b] * blurred[b * ROWS:(b + 1) * ROWS]
        resid = inv_ref[q, :, cols].astype(F32) * (model - obs_ref[q, :, cols])
        for b in range(NB):
            at = b * ROWS if b < 4 else 640 + (b - 4) * ROWS
            wide[at:at + ROWS, cols] = (coef[b] * resid).astype(BF)
        return carry

    lax.fori_loop(0, WIDTH // nc, chunk, 0)


def adjoint_step(q, adj, wide, back_ref):
    head, rest = wide[0:128, :], wide[640:704, :]
    for c in range(1, 5):
        wide[c * 128:(c + 1) * 128, :] = jnp.concatenate([jnp.zeros((128, c), BF), head[:, :SPAN - c]], axis=1)
        wide[640 + c * 64:640 + (c + 1) * 64, :] = jnp.concatenate([jnp.zeros((64, c), BF), rest[:, :SPAN - c]], axis=1)
    part = jnp.dot(adj[...], wide[...], preferred_element_type=F32)
    back = part[0:TALL]
    for a in range(1, 5):
        back = back + pltpu.roll(part[a * TALL:(a + 1) * TALL], 5 * a, axis=1)
    for c in range(NCH):
        back_ref[c, q] = back[:, c * LANES:(c + 1) * LANES].astype(BF)


SINGLE = ((0,), (1,), (2,), (3,))
GROUPS = {1: SINGLE, 2: SINGLE, 3: SINGLE, 4: SINGLE, 5: SINGLE, 6: SINGLE, 7: SINGLE}
TURNS = (0, 4, 8, 12)
ORDER = (
    (1, 0), (1, 1), (1, 2), (1, 3), (2, 0), (2, 1), (3, 0), (2, 2), (3, 1), (2, 3), (3, 2), (4, 0), (5, 0), (3, 3), (4, 1), (5, 1),
    (6, 0), (4, 2), (5, 2), (6, 1), (7, 0), (4, 3), (5, 3), (6, 2), (7, 1), (6, 3), (7, 2), (7, 3),
)


def group_of(step, q):
    for n, group in enumerate(GROUPS[step]):
        if q in group:
            return n, group.index(q)


def fused_kernel(foot_hbm, offs_hbm, slots_hbm, kernels, sky_hbm, coefs_hbm, obs_hbm, inv_hbm, pieces, target, *scratch):
    scratch = list(scratch)
    take = lambda count: [scratch.pop(0) for _ in range(count)]
    recv1, recv2, recv4 = take(len(GROUPS[1])), take(len(GROUPS[2])), take(len(GROUPS[5]))
    recv5, tiles = take(len(GROUPS[6])), take(NV)
    (foot, offs, slots, kt, fwd, adj, sky, coef, obs, inv, stage1, stage2, stage3, stage5, stage6, band, back, stack, wide,
     s1, r1, s2, r2, s3, r3, s4, r4, s5, r5, s6, r6, loads) = scratch
    me_e, me_p = lax.axis_index(E_AXIS), lax.axis_index(P_AXIS)
    first_loads = [
        pltpu.make_async_copy(src, dst, loads.at[k])
        for k, (src, dst) in enumerate(((foot_hbm, foot), (offs_hbm, offs), (slots_hbm, slots), (sky_hbm, sky)), 3)
    ]
    rest_loads = [
        pltpu.make_async_copy(src, dst, loads.at[k])
        for k, (src, dst) in enumerate(((coefs_hbm, coef), (obs_hbm, obs), (inv_hbm, inv)))
    ]
    for load in first_loads:
        load.start()
    barrier = pltpu.get_barrier_semaphore()
    for d in range(1, NE):
        pl.semaphore_signal(barrier, inc=1, device_id=(lax.rem(me_e + d, NE), me_p), device_id_type=MESH_ID)
    for d in range(1, NP):
        pl.semaphore_signal(barrier, inc=1, device_id=(me_e, lax.rem(me_p + d, NP)), device_id_type=MESH_ID)
    for load in first_loads:
        load.wait()
    for load in rest_loads:
        load.start()

    def fill(g, carry):
        for q in range(NV):
            base = jnp.where(me_p < (offs[0, 4 * g + q] >> 5), 4, 0)
            local, found = jnp.int32(0), jnp.int32(-1)
            for j in range(4):
                slot = slots[foot[base + j, 4 * g + q]]
                local = jnp.where((slot >> 6) == me_e, slot & 63, local)
                found = jnp.where((slot >> 6) == me_e, slot & 63, found)
            stage1[g, q] = sky[local]
            target[4 * g + q] = found
        return carry

    lax.fori_loop(0, NE, fill, 0)
    phase = [offs[0, 4 * me_e + q] >> 5 for q in range(NV)]
    shift = [offs[1, 4 * me_e + q] - RIM for q in range(NV)]
    source = []
    for q in range(NV):
        base = jnp.where(me_p < phase[q], 4, 0)
        source.append([slots[foot[base + j, 4 * me_e + q]] >> 6 for j in range(4)])
    pl.semaphore_wait(barrier, NE + NP - 2)

    sent = []

    def guarded(condition, action):
        if condition is None:
            action()
        else:
            pl.when(condition)(action)

    def exchange(count, me, device, src, dst, send, recv, sends=None, receives=None):
        inward = []
        for d in range(1, count):
            to, of = lax.rem(me + d, count), lax.rem(me + count - d, count)

            def make(slot, to=to):
                return pltpu.make_async_remote_copy(
                    src_ref=src(to), dst_ref=dst(slot), send_sem=send.at[to], recv_sem=recv.at[slot],
                    device_id=device(to), device_id_type=MESH_ID)

            go = None if sends is None else sends(to)
            come = None if receives is None else receives(of)
            guarded(go, lambda make=make: make(me).start())
            sent.append((go, lambda make=make: make(me).wait_send()))
            inward.append((come, lambda make=make, of=of: make(of).wait_recv()))
        return inward

    over_e, over_p = (lambda to: (to, me_p)), (lambda to: (me_e, to))

    def arrive(copies):
        for condition, action in copies:
            guarded(condition, action)

    def turn_of(group):
        return TURNS[group[0]]

    def chunk_at(device, turn):
        return jnp.minimum(chunk_of(device, turn), NCH - 1)

    def holds(turn):
        return lambda device: chunk_of(device, turn) < NCH

    def mine(turn):
        return lambda device: chunk_of(me_p, turn) < NCH

    def span(group):
        return pl.ds(group[0], len(group))

    def step1(n, group):
        qs = span(group)
        recv1[n][me_e] = stage1[me_e, group[0]:group[0] + len(group)]
        return exchange(NE, me_e, over_e, lambda to: stage1.at[to, qs], lambda i: recv1[n].at[i], s1.at[n], r1.at[n])

    def step2(n, group):
        qs, turn = span(group), turn_of(group)
        for q in group:
            m, k = group_of(1, q)
            row = jnp.concatenate([recv1[m][source[q][j], k] for j in range(4)], axis=1).astype(F32)
            row = pltpu.roll(row, (FULL - shift[q]) & (FULL - 1), axis=1)[:, :SPAN].astype(BF)
            for c in range(NCH):
                stage2[c, q] = row[:, c * LANES:(c + 1) * LANES]

        @pl.when(mine(turn)(me_p))
        def _():
            recv2[n][me_p] = stage2[chunk_at(me_p, turn), group[0]:group[0] + len(group)]

        return exchange(
            NP, me_p, over_p, lambda to: stage2.at[chunk_at(to, turn), qs], lambda i: recv2[n].at[i], s2.at[n], r2.at[n],
            holds(turn), mine(turn))

    def step3(n, group):
        qs, turn = span(group), turn_of(group)

        @pl.when(mine(turn)(me_p))
        def _():
            for q in group:
                m, k = group_of(2, q)
                for to in range(NP):
                    strip = (phase[q] + to) & 15
                    stage3[to, q, 16:48] = recv2[m][strip, k]
                    if to > 0:
                        stage3[to, q, 0:16] = recv2[m][(strip + 15) & 15, k, 16:32]
                    else:
                        stage3[to, q, 0:16] = jnp.zeros((16, LANES), BF)
                    if to < NP - 1:
                        stage3[to, q, 48:64] = recv2[m][(strip + 1) & 15, k, 0:16]
                    else:
                        stage3[to, q, 48:64] = jnp.zeros((16, LANES), BF)
                band[chunk_at(me_p, turn), q] = stage3[me_p, q]

        return exchange(
            NP, me_p, over_p, lambda to: stage3.at[to, qs], lambda i: band.at[chunk_at(i, turn), qs], s3.at[n],
            r3.at[n], mine(turn), holds(turn))

    def step4(n, group):
        for q in group:
            forward_step(q, band, coef, obs, inv, fwd, stack, wide)

    def step5(n, group):
        qs, turn = span(group), turn_of(group)
        for q in group:
            adjoint_step(q, adj, wide, back)

        @pl.when(mine(turn)(me_p))
        def _():
            recv4[n][me_p] = back[chunk_at(me_p, turn), group[0]:group[0] + len(group)]

        return exchange(
            NP, me_p, over_p, lambda to: back.at[chunk_at(to, turn), qs], lambda i: recv4[n].at[i], s4.at[n],
            r4.at[n], holds(turn), mine(turn))

    def step6(n, group):
        qs, turn = span(group), turn_of(group)

        def sums():
            for q in group:
                m, k = group_of(5, q)
                for to in range(NP):
                    strip = (to - phase[q]) & 15
                    centre = recv4[m][strip, k, 16:48].astype(F32)
                    above = jnp.where(strip > 0, recv4[m][(strip + 15) & 15, k, 48:64].astype(F32), 0.0)
                    below = jnp.where(strip < NP - 1, recv4[m][(strip + 1) & 15, k, 0:16].astype(F32), 0.0)
                    stage5[to, q, 0:16] = (centre[0:16] + above).astype(BF)
                    stage5[to, q, 16:32] = (centre[16:32] + below).astype(BF)
                recv5[n][chunk_at(me_p, turn), group.index(q)] = stage5[me_p, q]

        pl.when(mine(turn)(me_p))(sums)
        return exchange(
            NP, me_p, over_p, lambda to: stage5.at[to, qs], lambda i: recv5[n].at[chunk_at(i, turn)], s5.at[n],
            r5.at[n], mine(turn), holds(turn))

    def step7(n, group):
        qs = span(group)
        for q in group:
            m, k = group_of(6, q)
            parts = [recv5[m][c, k].astype(F32) for c in range(NCH)]
            row = jnp.concatenate(parts + [jnp.zeros((ROWS, FULL - SPAN), F32)], axis=1)
            row = pltpu.roll(row, shift[q], axis=1).astype(BF)
            for j in range(4):
                tiles[q][j] = row[:, j * 512:(j + 1) * 512]
            for o in range(NE):
                which = jnp.int32(0)
                for j in range(1, 4):
                    which = jnp.where(source[q][j] == o, j, which)
                stage6[o, q] = tiles[q][which]
            pieces[me_e, q] = stage6[me_e, q]
        return exchange(NE, me_e, over_e, lambda to: stage6.at[to, qs], lambda i: pieces.at[i, qs], s6.at[n], r6.at[n])

    steps = (step1, step2, step3, step4, step5, step6, step7)
    waiting = {}
    for n, g in ORDER:
        if (n, g) == (2, 0):
            build_tables(kernels, kt, fwd, adj)
        if (n, g) == (4, 0):
            for load in rest_loads:
                load.wait()
        group = GROUPS[n][g]
        for q in group:
            before = (n - 1, group_of(n - 1, q)[0]) if n > 1 else None
            if before in waiting:
                arrive(waiting.pop(before))
        copies = steps[n - 1](g, group)
        if copies is not None:
            waiting[n, g] = copies
    for key in sorted(waiting):
        arrive(waiting[key])
    arrive(sent)


def fused(footprints, offsets, tile_slot, kernels, sky, coefs, observed, inv_var):
    dma = pltpu.SemaphoreType.DMA
    smem = pl.BlockSpec(memory_space=pltpu.SMEM)
    vmem = pl.BlockSpec(memory_space=pltpu.VMEM)
    hbm = pl.BlockSpec(memory_space=pl.ANY)
    size = lambda n: [len(group) for group in GROUPS[n]]
    shapes = [(NE, k, ROWS, 512) for k in size(1)] + [(NP, k, ROWS, LANES) for k in size(2)]
    shapes += [(NP, k, TALL, LANES) for k in size(5)] + [(NCH, k, ROWS, LANES) for k in size(6)] + [(4, ROWS, 512)] * NV
    return pl.pallas_call(
        fused_kernel,
        out_shape=(jax.ShapeDtypeStruct((NE, NV, ROWS, 512), BF), jax.ShapeDtypeStruct((NE * NV,), jnp.int32)),
        in_specs=[hbm, hbm, hbm, vmem, hbm, hbm, hbm, hbm],
        out_specs=(vmem, smem),
        scratch_shapes=[pltpu.VMEM(s, BF) for s in shapes]
        + [
            pltpu.SMEM(footprints.shape, jnp.int32),
            pltpu.SMEM(offsets.shape, jnp.int32),
            pltpu.SMEM(tile_slot.shape, jnp.int32),
            pltpu.VMEM((NB, ROWS, LANES), F32),
            pltpu.VMEM((NB * ROWS, KS * TALL), BF),
            pltpu.VMEM((5 * TALL, 5 * NB * ROWS), BF),
            pltpu.VMEM(sky.shape, BF),
            pltpu.VMEM(coefs.shape, BF),
            pltpu.VMEM(observed.shape, F32),
            pltpu.VMEM(inv_var.shape, BF),
            pltpu.VMEM((NE, NV, ROWS, 512), BF),
            pltpu.VMEM((NCH, NV, ROWS, LANES), BF),
            pltpu.VMEM((NP, NV, TALL, LANES), BF),
            pltpu.VMEM((NP, NV, ROWS, LANES), BF),
            pltpu.VMEM((NE, NV, ROWS, 512), BF),
            pltpu.VMEM((NCH, NV, TALL, LANES), BF),
            pltpu.VMEM((NCH, NV, TALL, LANES), BF),
            pltpu.VMEM((KS * TALL, WIDTH), BF),
            pltpu.VMEM((5 * NB * ROWS, SPAN), BF),
        ]
        + [dma((len(GROUPS[n]), NE if n in (1, 7) else NP)) for n in (1, 2, 3, 5, 6, 7) for _ in range(2)] + [dma((7,))],
        compiler_params=pltpu.CompilerParams(collective_id=0, has_side_effects=True, vmem_limit_bytes=VLIM),
        name="fused",
    )(footprints, offsets, tile_slot, kernels, sky, coefs, observed, inv_var)


VLIM = 60 * 2**20


def total_kernel(target, pieces, out):
    step = pl.program_id(0)
    out[...] = jnp.zeros(out.shape, F32)
    count = out.shape[0]

    def add(e, carry):
        at = target[e] - step * count

        @pl.when((at >= 0) & (at < count))
        def _():
            out[at] = out[at] + pieces[e].astype(F32)

        return carry

    lax.fori_loop(0, NE * NV, add, 0)


def total(target, pieces, shape):
    pieces = pieces.reshape(NE * NV, ROWS, 512)
    return pl.pallas_call(
        total_kernel,
        grid=(4,),
        out_shape=jax.ShapeDtypeStruct(shape, F32),
        in_specs=[pl.BlockSpec(memory_space=pltpu.SMEM), pl.BlockSpec(pieces.shape, lambda i: (0, 0, 0))],
        out_specs=pl.BlockSpec((shape[0] // 4,) + shape[1:], lambda i: (i, 0, 0)),
        compiler_params=pltpu.CompilerParams(vmem_limit_bytes=VLIM),
        name="total",
    )(target, pieces)


def local(sky, kernels, coefs, observed, inv_var, footprints, offsets, tile_slot):
    pieces, target = fused(footprints.T, offsets.T, tile_slot, kernels, sky, coefs, observed, inv_var)
    return total(target, pieces, sky.shape)


def solution(mesh):
    return jax.shard_map(
        local,
        mesh=mesh,
        in_specs=(
            P("exp", "pix", None),
            P(),
            P("exp", None, "pix", None),
            P("exp", "pix", None),
            P("exp", "pix", None),
            P(),
            P(),
            P(),
        ),
        out_specs=P("exp", "pix", None),
        check_vma=False,
    )
```

```python
import jax
import jax.numpy as jnp
from jax import lax
from jax.experimental import pallas as pl
from jax.experimental.pallas import tpu as pltpu
from jax.sharding import PartitionSpec as P

E_AXIS, P_AXIS = "exp", "pix"
MESH_ID = pl.DeviceIdType.MESH
KS, NB, RIM, NV = 25, 6, 12, 4
NE, NP = 8, 16
ROWS, TALL, LANES = 32, 64, 128
WIDTH, SPAN, FULL, NCH = 1536, 1664, 2048, 13
BF, F32 = jnp.bfloat16, jnp.float32


def build_tables(kernels, kt, fwd, adj):
    lane = lax.broadcasted_iota(jnp.int32, (ROWS, LANES), 1)
    for b in range(NB):
        square = jnp.concatenate([kernels[b].astype(F32), jnp.zeros((KS, LANES - KS), F32)], axis=1)
        square = jnp.concatenate([square, jnp.zeros((LANES - KS, LANES), F32)], axis=0)
        kt[b] = pltpu.roll(square.T[0:ROWS], 4, axis=1)
    tail = {}
    for m in range(13):
        blocks = []
        for b in range(NB):
            low = pltpu.roll(jnp.broadcast_to(kt[b, 2 * m:2 * m + 1, :], (ROWS, LANES)), 0, axis=1, stride=1, stride_axis=0)
            if 2 * m + 1 < KS:
                high = pltpu.roll(
                    jnp.broadcast_to(kt[b, 2 * m + 1:2 * m + 2, :], (ROWS, LANES)), TALL, axis=1, stride=1, stride_axis=0
                )
                block = jnp.where(lane < TALL, low, high)
                fwd[b * ROWS:(b + 1) * ROWS, m * LANES:(m + 1) * LANES] = block.astype(BF)
            else:
                block = low
                fwd[b * ROWS:(b + 1) * ROWS, m * LANES:m * LANES + TALL] = block[:, :TALL].astype(BF)
            blocks.append(block)
        turned_a = jnp.concatenate(blocks[:4], axis=0).T
        turned_b = jnp.concatenate(blocks[4:] + [jnp.zeros((2 * ROWS, LANES), F32)], axis=0).T
        for h in range(2):
            v = 2 * m + h
            if v < KS:
                a, c = divmod(v, 5)
                adj[a * TALL:(a + 1) * TALL, c * LANES:(c + 1) * LANES] = turned_a[h * TALL:(h + 1) * TALL].astype(BF)
                tail[a, c] = turned_b[h * TALL:(h + 1) * TALL]
    wide_lane = lax.broadcasted_iota(jnp.int32, (TALL, LANES), 1)
    for a in range(5):
        for c in (0, 2):
            pair = jnp.where(wide_lane < 64, tail[a, c], pltpu.roll(tail[a, c + 1], 64, axis=1))
            adj[a * TALL:(a + 1) * TALL, 640 + c * 64:640 + c * 64 + LANES] = pair.astype(BF)
        adj[a * TALL:(a + 1) * TALL, 896:960] = tail[a, 4][:, :64].astype(BF)


def chunk_of(device, turn):
    return lax.rem(device + 2 * NP - turn, NP)


def forward_step(q, band, coef_ref, obs_ref, inv_ref, fwd, stack, wide):
    win = jnp.concatenate([band[c, q] for c in range(NCH)], axis=1)
    for v in range(KS):
        stack[v * TALL:(v + 1) * TALL, :] = win[:, v:v + WIDTH]
    nc = 512
    wide[0:128, WIDTH:] = jnp.zeros((128, SPAN - WIDTH), BF)
    wide[640:704, WIDTH:] = jnp.zeros((64, SPAN - WIDTH), BF)

    def chunk(n, carry):
        cols = pl.ds(pl.multiple_of(n * nc, nc), nc)
        blurred = jnp.dot(fwd[...], stack[:, cols], preferred_element_type=F32)
        coef = [coef_ref[q, b, :, cols].astype(F32) for b in range(NB)]
        model = coef[0] * blurred[0:ROWS]
        for b in range(1, NB):
            model = model + coef[b] * blurred[b * ROWS:(b + 1) * ROWS]
        resid = inv_ref[q, :, cols].astype(F32) * (model - obs_ref[q, :, cols])
        for b in range(NB):
            at = b * ROWS if b < 4 else 640 + (b - 4) * ROWS
            wide[at:at + ROWS, cols] = (coef[b] * resid).astype(BF)
        return carry

    lax.fori_loop(0, WIDTH // nc, chunk, 0)


def adjoint_step(q, adj, wide, back_ref):
    head, rest = wide[0:128, :], wide[640:704, :]
    for c in range(1, 5):
        wide[c * 128:(c + 1) * 128, :] = jnp.concatenate([jnp.zeros((128, c), BF), head[:, :SPAN - c]], axis=1)
        wide[640 + c * 64:640 + (c + 1) * 64, :] = jnp.concatenate([jnp.zeros((64, c), BF), rest[:, :SPAN - c]], axis=1)
    part = jnp.dot(adj[...], wide[...], preferred_element_type=F32)
    back = part[0:TALL]
    for a in range(1, 5):
        back = back + pltpu.roll(part[a * TALL:(a + 1) * TALL], 5 * a, axis=1)
    for c in range(NCH):
        back_ref[c, q] = back[:, c * LANES:(c + 1) * LANES].astype(BF)


SINGLE = ((0,), (1,), (2,), (3,))
GROUPS = {1: SINGLE, 2: SINGLE, 3: SINGLE, 4: SINGLE, 5: SINGLE, 6: SINGLE, 7: SINGLE}
TURNS = (0, 4, 8, 12)
HOPS_E = (4, 2, 6, 3, 5, 7, 1)
HOPS_P = (
    (1, 0), (0, 1), (3, 0), (0, 3), (1, 2), (2, 1), (3, 2), (2, 3), (2, 0), (0, 2), (1, 1), (3, 3), (1, 3), (3, 1), (2, 2),
)
ORDER = (
    (1, 0), (1, 1), (1, 2), (1, 3), (2, 0), (2, 1), (3, 0), (2, 2), (3, 1), (2, 3), (3, 2), (4, 0), (5, 0), (3, 3), (4, 1), (5, 1),
    (6, 0), (4, 2), (5, 2), (6, 1), (7, 0), (4, 3), (5, 3), (6, 2), (7, 1), (6, 3), (7, 2), (7, 3),
)


def group_of(step, q):
    for n, group in enumerate(GROUPS[step]):
        if q in group:
            return n, group.index(q)


def fused_kernel(foot_hbm, offs_hbm, slots_hbm, kernels, sky_hbm, coefs_hbm, obs_hbm, inv_hbm, pieces, target, *scratch):
    scratch = list(scratch)
    take = lambda count: [scratch.pop(0) for _ in range(count)]
    recv1, recv2, recv4 = take(len(GROUPS[1])), take(len(GROUPS[2])), take(len(GROUPS[5]))
    recv5, tiles = take(len(GROUPS[6])), take(NV)
    (foot, offs, slots, kt, fwd, adj, sky, coef, obs, inv, stage1, stage2, stage3, stage5, stage6, band, back, stack, wide,
     s1, r1, s2, r2, s3, r3, s4, r4, s5, r5, s6, r6, loads) = scratch
    me_e, me_p = lax.axis_index(E_AXIS), lax.axis_index(P_AXIS)
    first_loads = [
        pltpu.make_async_copy(src, dst, loads.at[k])
        for k, (src, dst) in enumerate(((foot_hbm, foot), (offs_hbm, offs), (slots_hbm, slots), (sky_hbm, sky)), 3)
    ]
    rest_loads = [
        pltpu.make_async_copy(src, dst, loads.at[k])
        for k, (src, dst) in enumerate(((coefs_hbm, coef), (obs_hbm, obs), (inv_hbm, inv)))
    ]
    for load in first_loads:
        load.start()
    barrier = pltpu.get_barrier_semaphore()
    for d in range(1, NE):
        pl.semaphore_signal(barrier, inc=1, device_id=(lax.rem(me_e + d, NE), me_p), device_id_type=MESH_ID)
    for d in range(1, NP):
        pl.semaphore_signal(barrier, inc=1, device_id=(me_e, lax.rem(me_p + d, NP)), device_id_type=MESH_ID)
    for load in first_loads:
        load.wait()
    for load in rest_loads:
        load.start()

    def fill(g, carry):
        for q in range(NV):
            base = jnp.where(me_p < (offs[0, 4 * g + q] >> 5), 4, 0)
            local, found = jnp.int32(0), jnp.int32(-1)
            for j in range(4):
                slot = slots[foot[base + j, 4 * g + q]]
                local = jnp.where((slot >> 6) == me_e, slot & 63, local)
                found = jnp.where((slot >> 6) == me_e, slot & 63, found)
            stage1[g, q] = sky[local]
            target[4 * g + q] = found
        return carry

    lax.fori_loop(0, NE, fill, 0)
    phase = [offs[0, 4 * me_e + q] >> 5 for q in range(NV)]
    shift = [offs[1, 4 * me_e + q] - RIM for q in range(NV)]
    source = []
    for q in range(NV):
        base = jnp.where(me_p < phase[q], 4, 0)
        source.append([slots[foot[base + j, 4 * me_e + q]] >> 6 for j in range(4)])
    pl.semaphore_wait(barrier, NE + NP - 2)

    sent = []

    def guarded(condition, action):
        if condition is None:
            action()
        else:
            pl.when(condition)(action)

    def taken(view, sem, counts):
        def wait(count):
            pltpu.make_async_copy(view(count), view(count), sem).wait()

        return [(condition, lambda count=count: wait(count)) for condition, count in counts]

    def exchange(partners, src, dst, send, recv, outward, inward, sends=None):
        for to, device in partners:
            def start(to=to, device=device):
                pltpu.make_async_remote_copy(
                    src_ref=src(to), dst_ref=dst, send_sem=send, recv_sem=recv,
                    device_id=device, device_id_type=MESH_ID).start()

            guarded(None if sends is None else sends(to), start)
        sent.extend(taken(outward[0], send, outward[1]))
        return taken(inward[0], recv, inward[1])

    column, row_at = me_p // 4, lax.rem(me_p, 4)
    exp_partners, pix_partners = [], []
    for d in HOPS_E:
        to = lax.rem(me_e + d, NE)
        exp_partners.append((to, (to, me_p)))
    for dx, dy in HOPS_P:
        to = lax.rem(column + dx, 4) * 4 + lax.rem(row_at + dy, 4)
        pix_partners.append((to, (me_e, to)))

    def arrive(copies):
        for condition, action in copies:
            guarded(condition, action)

    def turn_of(group):
        return TURNS[group[0]]

    def chunk_at(device, turn):
        return jnp.minimum(chunk_of(device, turn), NCH - 1)

    def holds(turn):
        return lambda device: chunk_of(device, turn) < NCH

    def mine(turn):
        return lambda device: chunk_of(me_p, turn) < NCH

    def to_all(turn):
        return [(mine(turn)(me_p), NP - 1)]

    def to_holders(turn):
        return [(mine(turn)(me_p), NCH - 1), (jnp.logical_not(mine(turn)(me_p)), NCH)]

    def span(group):
        return pl.ds(group[0], len(group))

    def step1(n, group):
        qs = span(group)
        recv1[n][me_e] = stage1[me_e, group[0]:group[0] + len(group)]
        return exchange(
            exp_partners, lambda to: stage1.at[to, qs], recv1[n].at[me_e], s1.at[n], r1.at[n],
            (lambda k: stage1.at[pl.ds(0, k), qs], [(None, NE - 1)]), (lambda k: recv1[n].at[pl.ds(0, k)], [(None, NE - 1)]))

    def step2(n, group):
        qs, turn = span(group), turn_of(group)
        for q in group:
            m, k = group_of(1, q)
            row = jnp.concatenate([recv1[m][source[q][j], k] for j in range(4)], axis=1).astype(F32)
            row = pltpu.roll(row, (FULL - shift[q]) & (FULL - 1), axis=1)[:, :SPAN].astype(BF)
            for c in range(NCH):
                stage2[c, q] = row[:, c * LANES:(c + 1) * LANES]

        @pl.when(mine(turn)(me_p))
        def _():
            recv2[n][me_p] = stage2[chunk_at(me_p, turn), group[0]:group[0] + len(group)]

        return exchange(
            pix_partners, lambda to: stage2.at[chunk_at(to, turn), qs], recv2[n].at[me_p], s2.at[n], r2.at[n],
            (lambda k: stage2.at[pl.ds(0, k), qs], to_holders(turn)), (lambda k: recv2[n].at[pl.ds(0, k)], to_all(turn)),
            holds(turn))

    def step3(n, group):
        qs, turn = span(group), turn_of(group)

        @pl.when(mine(turn)(me_p))
        def _():
            for q in group:
                m, k = group_of(2, q)
                for to in range(NP):
                    strip = (phase[q] + to) & 15
                    stage3[to, q, 16:48] = recv2[m][strip, k]
                    if to > 0:
                        stage3[to, q, 0:16] = recv2[m][(strip + 15) & 15, k, 16:32]
                    else:
                        stage3[to, q, 0:16] = jnp.zeros((16, LANES), BF)
                    if to < NP - 1:
                        stage3[to, q, 48:64] = recv2[m][(strip + 1) & 15, k, 0:16]
                    else:
                        stage3[to, q, 48:64] = jnp.zeros((16, LANES), BF)
                band[chunk_at(me_p, turn), q] = stage3[me_p, q]

        return exchange(
            pix_partners, lambda to: stage3.at[to, qs], band.at[chunk_at(me_p, turn), qs], s3.at[n], r3.at[n],
            (lambda k: stage3.at[pl.ds(0, k), qs], to_all(turn)), (lambda k: band.at[pl.ds(0, k), qs], to_holders(turn)),
            mine(turn))

    def step4(n, group):
        for q in group:
            forward_step(q, band, coef, obs, inv, fwd, stack, wide)

    def step5(n, group):
        qs, turn = span(group), turn_of(group)
        for q in group:
            adjoint_step(q, adj, wide, back)

        @pl.when(mine(turn)(me_p))
        def _():
            recv4[n][me_p] = back[chunk_at(me_p, turn), group[0]:group[0] + len(group)]

        return exchange(
            pix_partners, lambda to: back.at[chunk_at(to, turn), qs], recv4[n].at[me_p], s4.at[n], r4.at[n],
            (lambda k: back.at[pl.ds(0, k), qs], to_holders(turn)), (lambda k: recv4[n].at[pl.ds(0, k)], to_all(turn)),
            holds(turn))

    def step6(n, group):
        qs, turn = span(group), turn_of(group)

        def sums():
            for q in group:
                m, k = group_of(5, q)
                for to in range(NP):
                    strip = (to - phase[q]) & 15
                    centre = recv4[m][strip, k, 16:48].astype(F32)
                    above = jnp.where(strip > 0, recv4[m][(strip + 15) & 15, k, 48:64].astype(F32), 0.0)
                    below = jnp.where(strip < NP - 1, recv4[m][(strip + 1) & 15, k, 0:16].astype(F32), 0.0)
                    stage5[to, q, 0:16] = (centre[0:16] + above).astype(BF)
                    stage5[to, q, 16:32] = (centre[16:32] + below).astype(BF)
                recv5[n][chunk_at(me_p, turn), group.index(q)] = stage5[me_p, q]

        pl.when(mine(turn)(me_p))(sums)
        return exchange(
            pix_partners, lambda to: stage5.at[to, qs], recv5[n].at[chunk_at(me_p, turn)], s5.at[n], r5.at[n],
            (lambda k: stage5.at[pl.ds(0, k), qs], to_all(turn)), (lambda k: recv5[n].at[pl.ds(0, k)], to_holders(turn)),
            mine(turn))

    def step7(n, group):
        qs = span(group)
        for q in group:
            m, k = group_of(6, q)
            parts = [recv5[m][c, k].astype(F32) for c in range(NCH)]
            row = jnp.concatenate(parts + [jnp.zeros((ROWS, FULL - SPAN), F32)], axis=1)
            row = pltpu.roll(row, shift[q], axis=1).astype(BF)
            for j in range(4):
                tiles[q][j] = row[:, j * 512:(j + 1) * 512]
            for o in range(NE):
                which = jnp.int32(0)
                for j in range(1, 4):
                    which = jnp.where(source[q][j] == o, j, which)
                stage6[o, q] = tiles[q][which]
            pieces[me_e, q] = stage6[me_e, q]
        return exchange(
            exp_partners, lambda to: stage6.at[to, qs], pieces.at[me_e, qs], s6.at[n], r6.at[n],
            (lambda k: stage6.at[pl.ds(0, k), qs], [(None, NE - 1)]), (lambda k: pieces.at[pl.ds(0, k), qs], [(None, NE - 1)]))

    steps = (step1, step2, step3, step4, step5, step6, step7)
    waiting = {}
    for n, g in ORDER:
        if (n, g) == (2, 0):
            build_tables(kernels, kt, fwd, adj)
        if (n, g) == (4, 0):
            for load in rest_loads:
                load.wait()
        group = GROUPS[n][g]
        for q in group:
            before = (n - 1, group_of(n - 1, q)[0]) if n > 1 else None
            if before in waiting:
                arrive(waiting.pop(before))
        copies = steps[n - 1](g, group)
        if copies is not None:
            waiting[n, g] = copies
    for key in sorted(waiting):
        arrive(waiting[key])
    arrive(sent)


def fused(footprints, offsets, tile_slot, kernels, sky, coefs, observed, inv_var):
    dma = pltpu.SemaphoreType.DMA
    smem = pl.BlockSpec(memory_space=pltpu.SMEM)
    vmem = pl.BlockSpec(memory_space=pltpu.VMEM)
    hbm = pl.BlockSpec(memory_space=pl.ANY)
    size = lambda n: [len(group) for group in GROUPS[n]]
    shapes = [(NE, k, ROWS, 512) for k in size(1)] + [(NP, k, ROWS, LANES) for k in size(2)]
    shapes += [(NP, k, TALL, LANES) for k in size(5)] + [(NCH, k, ROWS, LANES) for k in size(6)] + [(4, ROWS, 512)] * NV
    return pl.pallas_call(
        fused_kernel,
        out_shape=(jax.ShapeDtypeStruct((NE, NV, ROWS, 512), BF), jax.ShapeDtypeStruct((NE * NV,), jnp.int32)),
        in_specs=[hbm, hbm, hbm, vmem, hbm, hbm, hbm, hbm],
        out_specs=(vmem, smem),
        scratch_shapes=[pltpu.VMEM(s, BF) for s in shapes]
        + [
            pltpu.SMEM(footprints.shape, jnp.int32),
            pltpu.SMEM(offsets.shape, jnp.int32),
            pltpu.SMEM(tile_slot.shape, jnp.int32),
            pltpu.VMEM((NB, ROWS, LANES), F32),
            pltpu.VMEM((NB * ROWS, KS * TALL), BF),
            pltpu.VMEM((5 * TALL, 5 * NB * ROWS), BF),
            pltpu.VMEM(sky.shape, BF),
            pltpu.VMEM(coefs.shape, BF),
            pltpu.VMEM(observed.shape, F32),
            pltpu.VMEM(inv_var.shape, BF),
            pltpu.VMEM((NE, NV, ROWS, 512), BF),
            pltpu.VMEM((NCH, NV, ROWS, LANES), BF),
            pltpu.VMEM((NP, NV, TALL, LANES), BF),
            pltpu.VMEM((NP, NV, ROWS, LANES), BF),
            pltpu.VMEM((NE, NV, ROWS, 512), BF),
            pltpu.VMEM((NCH, NV, TALL, LANES), BF),
            pltpu.VMEM((NCH, NV, TALL, LANES), BF),
            pltpu.VMEM((KS * TALL, WIDTH), BF),
            pltpu.VMEM((5 * NB * ROWS, SPAN), BF),
        ]
        + [dma((len(GROUPS[n]),)) for n in (1, 2, 3, 5, 6, 7) for _ in range(2)] + [dma((7,))],
        compiler_params=pltpu.CompilerParams(collective_id=0, has_side_effects=True, vmem_limit_bytes=VLIM),
        name="fused",
    )(footprints, offsets, tile_slot, kernels, sky, coefs, observed, inv_var)


VLIM = 60 * 2**20


def total_kernel(target, pieces, out):
    step = pl.program_id(0)
    out[...] = jnp.zeros(out.shape, F32)
    count = out.shape[0]

    def add(e, carry):
        at = target[e] - step * count

        @pl.when((at >= 0) & (at < count))
        def _():
            out[at] = out[at] + pieces[e].astype(F32)

        return carry

    lax.fori_loop(0, NE * NV, add, 0)


def total(target, pieces, shape):
    pieces = pieces.reshape(NE * NV, ROWS, 512)
    return pl.pallas_call(
        total_kernel,
        grid=(4,),
        out_shape=jax.ShapeDtypeStruct(shape, F32),
        in_specs=[pl.BlockSpec(memory_space=pltpu.SMEM), pl.BlockSpec(pieces.shape, lambda i: (0, 0, 0))],
        out_specs=pl.BlockSpec((shape[0] // 4,) + shape[1:], lambda i: (i, 0, 0)),
        compiler_params=pltpu.CompilerParams(vmem_limit_bytes=VLIM),
        name="total",
    )(target, pieces)


def local(sky, kernels, coefs, observed, inv_var, footprints, offsets, tile_slot):
    pieces, target = fused(footprints.T, offsets.T, tile_slot, kernels, sky, coefs, observed, inv_var)
    return total(target, pieces, sky.shape)


def solution(mesh):
    return jax.shard_map(
        local,
        mesh=mesh,
        in_specs=(
            P("exp", "pix", None),
            P(),
            P("exp", None, "pix", None),
            P("exp", "pix", None),
            P("exp", "pix", None),
            P(),
            P(),
            P(),
        ),
        out_specs=P("exp", "pix", None),
        check_vma=False,
    )
```

```python
import jax
import jax.numpy as jnp
from jax import lax
from jax.experimental import pallas as pl
from jax.experimental.pallas import tpu as pltpu
from jax.sharding import PartitionSpec as P

E_AXIS, P_AXIS = "exp", "pix"
MESH_ID = pl.DeviceIdType.MESH
KS, NB, RIM, NV = 25, 6, 12, 4
NE, NP = 8, 16
ROWS, TALL, LANES = 32, 64, 128
WIDTH, SPAN, FULL, NCH = 1536, 1664, 2048, 13
BF, F32 = jnp.bfloat16, jnp.float32


def build_tables(kernels, kt, fwd, adj):
    lane = lax.broadcasted_iota(jnp.int32, (ROWS, LANES), 1)
    for b in range(NB):
        square = jnp.concatenate([kernels[b].astype(F32), jnp.zeros((KS, LANES - KS), F32)], axis=1)
        square = jnp.concatenate([square, jnp.zeros((LANES - KS, LANES), F32)], axis=0)
        kt[b] = pltpu.roll(square.T[0:ROWS], 4, axis=1)
    tail = {}
    for m in range(13):
        blocks = []
        for b in range(NB):
            low = pltpu.roll(jnp.broadcast_to(kt[b, 2 * m:2 * m + 1, :], (ROWS, LANES)), 0, axis=1, stride=1, stride_axis=0)
            if 2 * m + 1 < KS:
                high = pltpu.roll(
                    jnp.broadcast_to(kt[b, 2 * m + 1:2 * m + 2, :], (ROWS, LANES)), TALL, axis=1, stride=1, stride_axis=0
                )
                block = jnp.where(lane < TALL, low, high)
                fwd[b * ROWS:(b + 1) * ROWS, m * LANES:(m + 1) * LANES] = block.astype(BF)
            else:
                block = low
                fwd[b * ROWS:(b + 1) * ROWS, m * LANES:m * LANES + TALL] = block[:, :TALL].astype(BF)
            blocks.append(block)
        turned_a = jnp.concatenate(blocks[:4], axis=0).T
        turned_b = jnp.concatenate(blocks[4:] + [jnp.zeros((2 * ROWS, LANES), F32)], axis=0).T
        for h in range(2):
            v = 2 * m + h
            if v < KS:
                a, c = divmod(v, 5)
                adj[a * TALL:(a + 1) * TALL, c * LANES:(c + 1) * LANES] = turned_a[h * TALL:(h + 1) * TALL].astype(BF)
                tail[a, c] = turned_b[h * TALL:(h + 1) * TALL]
    wide_lane = lax.broadcasted_iota(jnp.int32, (TALL, LANES), 1)
    for a in range(5):
        for c in (0, 2):
            pair = jnp.where(wide_lane < 64, tail[a, c], pltpu.roll(tail[a, c + 1], 64, axis=1))
            adj[a * TALL:(a + 1) * TALL, 640 + c * 64:640 + c * 64 + LANES] = pair.astype(BF)
        adj[a * TALL:(a + 1) * TALL, 896:960] = tail[a, 4][:, :64].astype(BF)


def chunk_of(device, turn):
    return lax.rem(device + 2 * NP - turn, NP)


def forward_step(q, band, coef_ref, obs_ref, inv_ref, fwd, stack, wide):
    win = jnp.concatenate([band[c, q] for c in range(NCH)], axis=1)
    for v in range(KS):
        stack[v * TALL:(v + 1) * TALL, :] = win[:, v:v + WIDTH]
    nc = 1536
    wide[0:128, WIDTH:] = jnp.zeros((128, SPAN - WIDTH), BF)
    wide[640:704, WIDTH:] = jnp.zeros((64, SPAN - WIDTH), BF)

    def chunk(n, carry):
        cols = pl.ds(pl.multiple_of(n * nc, nc), nc)
        blurred = jnp.dot(fwd[...], stack[:, cols], preferred_element_type=F32)
        coef = [coef_ref[q, b, :, cols].astype(F32) for b in range(NB)]
        model = coef[0] * blurred[0:ROWS]
        for b in range(1, NB):
            model = model + coef[b] * blurred[b * ROWS:(b + 1) * ROWS]
        resid = inv_ref[q, :, cols].astype(F32) * (model - obs_ref[q, :, cols])
        for b in range(NB):
            at = b * ROWS if b < 4 else 640 + (b - 4) * ROWS
            wide[at:at + ROWS, cols] = (coef[b] * resid).astype(BF)
        return carry

    lax.fori_loop(0, WIDTH // nc, chunk, 0)


def adjoint_step(q, adj, wide, back_ref):
    head, rest = wide[0:128, :], wide[640:704, :]
    for c in range(1, 5):
        wide[c * 128:(c + 1) * 128, :] = jnp.concatenate([jnp.zeros((128, c), BF), head[:, :SPAN - c]], axis=1)
        wide[640 + c * 64:640 + (c + 1) * 64, :] = jnp.concatenate([jnp.zeros((64, c), BF), rest[:, :SPAN - c]], axis=1)
    part = jnp.dot(adj[...], wide[...], preferred_element_type=F32)
    back = part[0:TALL]
    for a in range(1, 5):
        back = back + pltpu.roll(part[a * TALL:(a + 1) * TALL], 5 * a, axis=1)
    for c in range(NCH):
        back_ref[c, q] = back[:, c * LANES:(c + 1) * LANES].astype(BF)


SINGLE = ((0,), (1,), (2,), (3,))
GROUPS = {1: SINGLE, 2: SINGLE, 3: SINGLE, 4: SINGLE, 5: SINGLE, 6: SINGLE, 7: SINGLE}
TURNS = (0, 4, 8, 12)
HOPS_E = (4, 2, 6, 3, 5, 7, 1)
HOPS_P = (
    (1, 0), (0, 1), (3, 0), (0, 3), (1, 2), (2, 1), (3, 2), (2, 3), (2, 0), (0, 2), (1, 1), (3, 3), (1, 3), (3, 1), (2, 2),
)
ORDER = ((1, 0), (1, 1), (1, 2), (1, 3), (2, 0), (2, 1), (3, 0), (2, 2), (3, 1), (2, 3), (4, 0), (3, 2), (5, 0), (3, 3), (4, 1), (5, 1), (4, 2), (6, 0), (5, 2), (4, 3), (6, 1), (5, 3), (7, 0), (6, 2), (7, 1), (6, 3), (7, 2), (7, 3))


def group_of(step, q):
    for n, group in enumerate(GROUPS[step]):
        if q in group:
            return n, group.index(q)


def fused_kernel(foot_hbm, offs_hbm, slots_hbm, kernels, sky_hbm, coefs_hbm, obs_hbm, inv_hbm, pieces, target, *scratch):
    scratch = list(scratch)
    take = lambda count: [scratch.pop(0) for _ in range(count)]
    recv1, recv2, recv4 = take(len(GROUPS[1])), take(len(GROUPS[2])), take(len(GROUPS[5]))
    recv5, tiles = take(len(GROUPS[6])), take(NV)
    (foot, offs, slots, kt, fwd, adj, sky, coef, obs, inv, stage1, stage2, stage3, stage5, stage6, band, back, stack, wide,
     s1, r1, s2, r2, s3, r3, s4, r4, s5, r5, s6, r6, loads) = scratch
    me_e, me_p = lax.axis_index(E_AXIS), lax.axis_index(P_AXIS)
    first_loads = [
        pltpu.make_async_copy(src, dst, loads.at[k])
        for k, (src, dst) in enumerate(((foot_hbm, foot), (offs_hbm, offs), (slots_hbm, slots), (sky_hbm, sky)), 3)
    ]
    rest_loads = [
        pltpu.make_async_copy(src, dst, loads.at[k])
        for k, (src, dst) in enumerate(((coefs_hbm, coef), (obs_hbm, obs), (inv_hbm, inv)))
    ]
    for load in first_loads:
        load.start()
    barrier = pltpu.get_barrier_semaphore()
    for d in range(1, NE):
        pl.semaphore_signal(barrier, inc=1, device_id=(lax.rem(me_e + d, NE), me_p), device_id_type=MESH_ID)
    for d in range(1, NP):
        pl.semaphore_signal(barrier, inc=1, device_id=(me_e, lax.rem(me_p + d, NP)), device_id_type=MESH_ID)
    for load in first_loads:
        load.wait()
    for load in rest_loads:
        load.start()

    def fill(g, carry):
        for q in range(NV):
            base = jnp.where(me_p < (offs[0, 4 * g + q] >> 5), 4, 0)
            local, found = jnp.int32(0), jnp.int32(-1)
            for j in range(4):
                slot = slots[foot[base + j, 4 * g + q]]
                local = jnp.where((slot >> 6) == me_e, slot & 63, local)
                found = jnp.where((slot >> 6) == me_e, slot & 63, found)
            stage1[g, q] = sky[local]
            target[4 * g + q] = found
        return carry

    lax.fori_loop(0, NE, fill, 0)
    phase = [offs[0, 4 * me_e + q] >> 5 for q in range(NV)]
    shift = [offs[1, 4 * me_e + q] - RIM for q in range(NV)]
    source = []
    for q in range(NV):
        base = jnp.where(me_p < phase[q], 4, 0)
        source.append([slots[foot[base + j, 4 * me_e + q]] >> 6 for j in range(4)])
    pl.semaphore_wait(barrier, NE + NP - 2)

    sent = []

    def guarded(condition, action):
        if condition is None:
            action()
        else:
            pl.when(condition)(action)

    def taken(view, sem, counts):
        def wait(count):
            pltpu.make_async_copy(view(count), view(count), sem).wait()

        return [(condition, lambda count=count: wait(count)) for condition, count in counts]

    def exchange(partners, src, dst, send, recv, outward, inward, sends=None):
        for to, device in partners:
            def start(to=to, device=device):
                pltpu.make_async_remote_copy(
                    src_ref=src(to), dst_ref=dst, send_sem=send, recv_sem=recv,
                    device_id=device, device_id_type=MESH_ID).start()

            guarded(None if sends is None else sends(to), start)
        sent.extend(taken(outward[0], send, outward[1]))
        return taken(inward[0], recv, inward[1])

    column, row_at = me_p // 4, lax.rem(me_p, 4)
    exp_partners, pix_partners = [], []
    for d in HOPS_E:
        to = lax.rem(me_e + d, NE)
        exp_partners.append((to, (to, me_p)))
    for dx, dy in HOPS_P:
        to = lax.rem(column + dx, 4) * 4 + lax.rem(row_at + dy, 4)
        pix_partners.append((to, (me_e, to)))

    def arrive(copies):
        for condition, action in copies:
            guarded(condition, action)

    def turn_of(group):
        return TURNS[group[0]]

    def chunk_at(device, turn):
        return jnp.minimum(chunk_of(device, turn), NCH - 1)

    def holds(turn):
        return lambda device: chunk_of(device, turn) < NCH

    def mine(turn):
        return lambda device: chunk_of(me_p, turn) < NCH

    def to_all(turn):
        return [(mine(turn)(me_p), NP - 1)]

    def to_holders(turn):
        return [(mine(turn)(me_p), NCH - 1), (jnp.logical_not(mine(turn)(me_p)), NCH)]

    def span(group):
        return pl.ds(group[0], len(group))

    def step1(n, group):
        qs = span(group)
        recv1[n][me_e] = stage1[me_e, group[0]:group[0] + len(group)]
        return exchange(
            exp_partners, lambda to: stage1.at[to, qs], recv1[n].at[me_e], s1.at[n], r1.at[n],
            (lambda k: stage1.at[pl.ds(0, k), qs], [(None, NE - 1)]), (lambda k: recv1[n].at[pl.ds(0, k)], [(None, NE - 1)]))

    def step2(n, group):
        qs, turn = span(group), turn_of(group)
        for q in group:
            m, k = group_of(1, q)
            row = jnp.concatenate([recv1[m][source[q][j], k] for j in range(4)], axis=1).astype(F32)
            row = pltpu.roll(row, (FULL - shift[q]) & (FULL - 1), axis=1)[:, :SPAN].astype(BF)
            for c in range(NCH):
                stage2[c, q] = row[:, c * LANES:(c + 1) * LANES]

        @pl.when(mine(turn)(me_p))
        def _():
            recv2[n][me_p] = stage2[chunk_at(me_p, turn), group[0]:group[0] + len(group)]

        return exchange(
            pix_partners, lambda to: stage2.at[chunk_at(to, turn), qs], recv2[n].at[me_p], s2.at[n], r2.at[n],
            (lambda k: stage2.at[pl.ds(0, k), qs], to_holders(turn)), (lambda k: recv2[n].at[pl.ds(0, k)], to_all(turn)),
            holds(turn))

    def step3(n, group):
        qs, turn = span(group), turn_of(group)

        @pl.when(mine(turn)(me_p))
        def _():
            for q in group:
                m, k = group_of(2, q)
                for to in range(NP):
                    strip = (phase[q] + to) & 15
                    stage3[to, q, 16:48] = recv2[m][strip, k]
                    if to > 0:
                        stage3[to, q, 0:16] = recv2[m][(strip + 15) & 15, k, 16:32]
                    else:
                        stage3[to, q, 0:16] = jnp.zeros((16, LANES), BF)
                    if to < NP - 1:
                        stage3[to, q, 48:64] = recv2[m][(strip + 1) & 15, k, 0:16]
                    else:
                        stage3[to, q, 48:64] = jnp.zeros((16, LANES), BF)
                band[chunk_at(me_p, turn), q] = stage3[me_p, q]

        return exchange(
            pix_partners, lambda to: stage3.at[to, qs], band.at[chunk_at(me_p, turn), qs], s3.at[n], r3.at[n],
            (lambda k: stage3.at[pl.ds(0, k), qs], to_all(turn)), (lambda k: band.at[pl.ds(0, k), qs], to_holders(turn)),
            mine(turn))

    def step4(n, group):
        for q in group:
            forward_step(q, band, coef, obs, inv, fwd, stack, wide)

    def step5(n, group):
        qs, turn = span(group), turn_of(group)
        for q in group:
            adjoint_step(q, adj, wide, back)

        @pl.when(mine(turn)(me_p))
        def _():
            recv4[n][me_p] = back[chunk_at(me_p, turn), group[0]:group[0] + len(group)]

        return exchange(
            pix_partners, lambda to: back.at[chunk_at(to, turn), qs], recv4[n].at[me_p], s4.at[n], r4.at[n],
            (lambda k: back.at[pl.ds(0, k), qs], to_holders(turn)), (lambda k: recv4[n].at[pl.ds(0, k)], to_all(turn)),
            holds(turn))

    def step6(n, group):
        qs, turn = span(group), turn_of(group)

        def sums():
            for q in group:
                m, k = group_of(5, q)
                for to in range(NP):
                    strip = (to - phase[q]) & 15
                    centre = recv4[m][strip, k, 16:48].astype(F32)
                    above = jnp.where(strip > 0, recv4[m][(strip + 15) & 15, k, 48:64].astype(F32), 0.0)
                    below = jnp.where(strip < NP - 1, recv4[m][(strip + 1) & 15, k, 0:16].astype(F32), 0.0)
                    stage5[to, q, 0:16] = (centre[0:16] + above).astype(BF)
                    stage5[to, q, 16:32] = (centre[16:32] + below).astype(BF)
                recv5[n][chunk_at(me_p, turn), group.index(q)] = stage5[me_p, q]

        pl.when(mine(turn)(me_p))(sums)
        return exchange(
            pix_partners, lambda to: stage5.at[to, qs], recv5[n].at[chunk_at(me_p, turn)], s5.at[n], r5.at[n],
            (lambda k: stage5.at[pl.ds(0, k), qs], to_all(turn)), (lambda k: recv5[n].at[pl.ds(0, k)], to_holders(turn)),
            mine(turn))

    def step7(n, group):
        qs = span(group)
        for q in group:
            m, k = group_of(6, q)
            parts = [recv5[m][c, k].astype(F32) for c in range(NCH)]
            row = jnp.concatenate(parts + [jnp.zeros((ROWS, FULL - SPAN), F32)], axis=1)
            row = pltpu.roll(row, shift[q], axis=1).astype(BF)
            for j in range(4):
                tiles[q][j] = row[:, j * 512:(j + 1) * 512]
            for o in range(NE):
                which = jnp.int32(0)
                for j in range(1, 4):
                    which = jnp.where(source[q][j] == o, j, which)
                stage6[o, q] = tiles[q][which]
            pieces[me_e, q] = stage6[me_e, q]
        return exchange(
            exp_partners, lambda to: stage6.at[to, qs], pieces.at[me_e, qs], s6.at[n], r6.at[n],
            (lambda k: stage6.at[pl.ds(0, k), qs], [(None, NE - 1)]), (lambda k: pieces.at[pl.ds(0, k), qs], [(None, NE - 1)]))

    steps = (step1, step2, step3, step4, step5, step6, step7)
    waiting = {}
    for n, g in ORDER:
        if (n, g) == (2, 0):
            build_tables(kernels, kt, fwd, adj)
        if (n, g) == (4, 0):
            for load in rest_loads:
                load.wait()
        group = GROUPS[n][g]
        for q in group:
            before = (n - 1, group_of(n - 1, q)[0]) if n > 1 else None
            if before in waiting:
                arrive(waiting.pop(before))
        copies = steps[n - 1](g, group)
        if copies is not None:
            waiting[n, g] = copies
    for key in sorted(waiting):
        arrive(waiting[key])
    arrive(sent)


def fused(footprints, offsets, tile_slot, kernels, sky, coefs, observed, inv_var):
    dma = pltpu.SemaphoreType.DMA
    smem = pl.BlockSpec(memory_space=pltpu.SMEM)
    vmem = pl.BlockSpec(memory_space=pltpu.VMEM)
    hbm = pl.BlockSpec(memory_space=pl.ANY)
    size = lambda n: [len(group) for group in GROUPS[n]]
    shapes = [(NE, k, ROWS, 512) for k in size(1)] + [(NP, k, ROWS, LANES) for k in size(2)]
    shapes += [(NP, k, TALL, LANES) for k in size(5)] + [(NCH, k, ROWS, LANES) for k in size(6)] + [(4, ROWS, 512)] * NV
    return pl.pallas_call(
        fused_kernel,
        out_shape=(jax.ShapeDtypeStruct((NE, NV, ROWS, 512), BF), jax.ShapeDtypeStruct((NE * NV,), jnp.int32)),
        in_specs=[hbm, hbm, hbm, vmem, hbm, hbm, hbm, hbm],
        out_specs=(vmem, smem),
        scratch_shapes=[pltpu.VMEM(s, BF) for s in shapes]
        + [
            pltpu.SMEM(footprints.shape, jnp.int32),
            pltpu.SMEM(offsets.shape, jnp.int32),
            pltpu.SMEM(tile_slot.shape, jnp.int32),
            pltpu.VMEM((NB, ROWS, LANES), F32),
            pltpu.VMEM((NB * ROWS, KS * TALL), BF),
            pltpu.VMEM((5 * TALL, 5 * NB * ROWS), BF),
            pltpu.VMEM(sky.shape, BF),
            pltpu.VMEM(coefs.shape, BF),
            pltpu.VMEM(observed.shape, F32),
            pltpu.VMEM(inv_var.shape, BF),
            pltpu.VMEM((NE, NV, ROWS, 512), BF),
            pltpu.VMEM((NCH, NV, ROWS, LANES), BF),
            pltpu.VMEM((NP, NV, TALL, LANES), BF),
            pltpu.VMEM((NP, NV, ROWS, LANES), BF),
            pltpu.VMEM((NE, NV, ROWS, 512), BF),
            pltpu.VMEM((NCH, NV, TALL, LANES), BF),
            pltpu.VMEM((NCH, NV, TALL, LANES), BF),
            pltpu.VMEM((KS * TALL, WIDTH), BF),
            pltpu.VMEM((5 * NB * ROWS, SPAN), BF),
        ]
        + [dma((len(GROUPS[n]),)) for n in (1, 2, 3, 5, 6, 7) for _ in range(2)] + [dma((7,))],
        compiler_params=pltpu.CompilerParams(collective_id=0, has_side_effects=True, vmem_limit_bytes=VLIM),
        name="fused",
    )(footprints, offsets, tile_slot, kernels, sky, coefs, observed, inv_var)


VLIM = 60 * 2**20


def total_kernel(target, pieces, out):
    step = pl.program_id(0)
    out[...] = jnp.zeros(out.shape, F32)
    count = out.shape[0]

    def add(e, carry):
        at = target[e] - step * count

        @pl.when((at >= 0) & (at < count))
        def _():
            out[at] = out[at] + pieces[e].astype(F32)

        return carry

    lax.fori_loop(0, NE * NV, add, 0)


def total(target, pieces, shape):
    pieces = pieces.reshape(NE * NV, ROWS, 512)
    return pl.pallas_call(
        total_kernel,
        grid=(2,),
        out_shape=jax.ShapeDtypeStruct(shape, F32),
        in_specs=[pl.BlockSpec(memory_space=pltpu.SMEM), pl.BlockSpec(pieces.shape, lambda i: (0, 0, 0))],
        out_specs=pl.BlockSpec((shape[0] // 2,) + shape[1:], lambda i: (i, 0, 0)),
        compiler_params=pltpu.CompilerParams(vmem_limit_bytes=VLIM),
        name="total",
    )(target, pieces)


def local(sky, kernels, coefs, observed, inv_var, footprints, offsets, tile_slot):
    pieces, target = fused(footprints.T, offsets.T, tile_slot, kernels, sky, coefs, observed, inv_var)
    return total(target, pieces, sky.shape)


def solution(mesh):
    return jax.shard_map(
        local,
        mesh=mesh,
        in_specs=(
            P("exp", "pix", None),
            P(),
            P("exp", None, "pix", None),
            P("exp", "pix", None),
            P("exp", "pix", None),
            P(),
            P(),
            P(),
        ),
        out_specs=P("exp", "pix", None),
        check_vma=False,
    )
```
